128 devices in a mesh: gx: 16 (over x, z_hi, core), gy: 8 (over z_lo, y).
Axes of the slice: x: 4, y: 4, z: 4 (z_hi: 2, z_lo: 2; z = z_hi * 2 + z_lo), core: 2. Of those that a mesh axis runs over, the one named last changes fastest.
Arguments:
- features: bfloat16 [112, 168, 2016], P('gx', 'gy'), may hold values from -60 to 60
- labels: int32 [112, 168, 42], P('gx', 'gy'), may hold values 0 or 1
- gain_one: float32 [48], replicated, may hold values from 0.1 to 1.9
- gain_two: float32 [48], replicated, may hold values from 0.1 to 1.9
- w_qkv: bfloat16 [48, 144], replicated, may hold values from -0.875 to 0.875
- w_proj: bfloat16 [48, 48], replicated, may hold values from -0.875 to 0.875
- w_up: bfloat16 [48, 192], replicated, may hold values from -0.875 to 0.875
- w_down: bfloat16 [192, 48], replicated, may hold values from -0.4375 to 0.4375
- w_head: bfloat16 [48, 2], replicated, may hold values from -0.875 to 0.875
Outputs:
- grad_features: bfloat16 [112, 168, 2016], P('gx', 'gy')
- grad_qkv: float32 [48, 144], replicated
- grad_proj: float32 [48, 48], replicated
- grad_up: float32 [48, 192], replicated
- grad_down: float32 [192, 48], replicated
- grad_head: float32 [48, 2], replicated
The draws below stay inside these ranges and needn't reach their ends.
All inputs are finite; a program needn't handle non-finite values. No bound on the sum of `labels` on one device may be relied on, other than what follows from the above.
Results may differ from the reference program's by a relative error of at most 0.0056.
The reference program's roundings to bfloat16 on the way count: a program that leaves them out, or rounds other values in their place, can miss the bound.
Values may be sent and summed in bfloat16 or wider, within the bound.
A program may use at most 64 MiB of HBM per device.

```python
import math
import jax
import jax.numpy as jnp
from jax import lax

C = 48
HEADS = 3
FF = 192
WIN = 7
SHIFT = 3
DEPTH = 42
NX = 112
NY = 168
TOKENS = 790272
N_GY = 8


def draw_features(key, part):
    key = jax.random.fold_in(key, 11)
    first, second, third = jax.random.split(key, 3)
    shape = (NX, NY, DEPTH, C)
    base = jax.random.normal(first, shape, jnp.float32)
    scales = jnp.exp(jax.random.uniform(second, (NX, NY, DEPTH, 1), jnp.float32, 0.0, 1.0) * math.log(10.0))
    channel = jnp.exp(jax.random.uniform(third, (C,), jnp.float32, -0.6, 0.6))
    values = jnp.clip(base * scales * channel, -60.0, 60.0)
    return values.reshape(NX, NY, DEPTH * C).astype(jnp.bfloat16)


def plant(values, stream_key, smallest, top_value):
    spot = [jax.random.randint(jax.random.fold_in(stream_key, axis), (), 0, length) for axis, length in enumerate(values.shape)]
    main_axis = values.shape.index(max(values.shape))
    next_to = spot[:main_axis] + [(spot[main_axis] + 1) % values.shape[main_axis]] + spot[main_axis + 1:]
    return values.at[tuple(spot)].set(smallest).at[tuple(next_to)].set(top_value)


def centred(stream_key, extent, scale, limit, kind=jnp.bfloat16):
    return jnp.clip(scale * jax.random.normal(stream_key, extent, jnp.float32), -limit, limit).astype(kind)


def setup_inputs(seed: int = 0) -> dict:
    arg_keys = jax.random.split(jax.random.key(seed), 10)
    features = draw_features(jax.random.fold_in(arg_keys[9], 71), 0)
    labels = plant((jax.random.randint(arg_keys[1], (NX, NY, DEPTH), 0, 4) < 1).astype(jnp.int32), jax.random.fold_in(arg_keys[1], 1), 0, 1)
    gain_one = jnp.clip(1.0 + 0.18 * jax.random.normal(arg_keys[2], (C,), jnp.float32), 0.1, 1.9)
    gain_two = jnp.clip(1.0 + 0.18 * jax.random.normal(arg_keys[3], (C,), jnp.float32), 0.1, 1.9)
    w_qkv = centred(arg_keys[4], (C, 3 * C), C ** -0.5, 0.875)
    w_proj = centred(arg_keys[5], (C, C), C ** -0.5, 0.875)
    w_up = centred(arg_keys[6], (C, FF), C ** -0.5, 0.875)
    w_down = centred(arg_keys[7], (FF, C), FF ** -0.5, 0.4375)
    w_head = centred(arg_keys[8], (C, 2), C ** -0.5, 0.875)
    return {"features": features, "labels": labels, "gain_one": gain_one, "gain_two": gain_two, "w_qkv": w_qkv, "w_proj": w_proj, "w_up": w_up, "w_down": w_down, "w_head": w_head}


EPS = 1e-05
HI = lax.Precision.HIGHEST

def rounded(values):
    return lax.optimization_barrier(values.astype(jnp.bfloat16)).astype(jnp.float32)

def layer_norm(values, gain):
    centre = lax.optimization_barrier(jnp.mean(values, axis=-1, keepdims=True))
    spread = values - centre
    second = lax.optimization_barrier(jnp.mean(spread * spread, axis=-1, keepdims=True))
    return spread * lax.rsqrt(second + EPS) * gain

def attend(normed, region, w_qkv, w_proj):
    blocks, points, width = normed.shape
    head_dim = width // HEADS
    packed = rounded(jnp.einsum('bpc,cf->bpf', normed.astype(jnp.float32), w_qkv, precision=HI))
    packed = packed.reshape(blocks, points, 3, HEADS, head_dim)
    query = packed[:, :, 0]
    keys = packed[:, :, 1]
    value = packed[:, :, 2]
    scores = jnp.einsum('bphd,bqhd->bhpq', query, keys, precision=HI) * head_dim ** (-0.5)
    allowed = (region[:, :, None] == region[:, None, :])[:, None]
    raw = jnp.where(allowed, jnp.exp(scores), 0.0)
    weights = rounded(raw / lax.optimization_barrier(jnp.sum(raw, axis=-1, keepdims=True)))
    mixed = rounded(jnp.einsum('bhpq,bqhd->bphd', weights, value, precision=HI))
    mixed = mixed.reshape(blocks, points, width)
    return jnp.einsum('bpc,cf->bpf', mixed, w_proj, precision=HI).astype(jnp.bfloat16)

def finish(resid, attn_out, marks, gain_two, w_up, w_down, w_head):
    state = rounded(resid + attn_out.astype(jnp.float32))
    normed = rounded(layer_norm(state, gain_two))
    inner = rounded(jax.nn.gelu(jnp.einsum('...c,cf->...f', normed, w_up, precision=HI)))
    result = rounded(state + jnp.einsum('...c,cf->...f', inner, w_down, precision=HI))
    logits = jnp.einsum('...c,cf->...f', result, w_head, precision=HI)
    sign = 1.0 - 2.0 * marks.astype(jnp.float32)
    return jnp.sum(jax.nn.softplus((logits[..., 1] - logits[..., 0]) * sign))

def block_loss(resid, region, marks, gain_one, gain_two, w_qkv, w_proj, w_up, w_down, w_head):
    normed = layer_norm(resid, gain_one).astype(jnp.bfloat16)
    attn_out = attend(normed, region, w_qkv, w_proj)
    return finish(resid, attn_out, marks, gain_two, w_up, w_down, w_head)

def to_windows(values):
    size_x, size_y, size_z = values.shape[:3]
    rest = values.shape[3:]
    cut = values.reshape((size_x // WIN, WIN, size_y // WIN, WIN, size_z // WIN, WIN) + rest)
    order = (0, 2, 4, 1, 3, 5) + tuple(range(6, 6 + len(rest)))
    return cut.transpose(order).reshape((-1, WIN ** 3) + rest)

def from_windows(values, size_x, size_y, size_z):
    rest = values.shape[2:]
    cut = values.reshape((size_x // WIN, size_y // WIN, size_z // WIN, WIN, WIN, WIN) + rest)
    order = (0, 3, 1, 4, 2, 5) + tuple(range(6, 6 + len(rest)))
    return cut.transpose(order).reshape((size_x, size_y, size_z) + rest)

def region_ids(count, total):
    place = jnp.arange(count, dtype=jnp.int32)
    return (place >= total - WIN).astype(jnp.int32) + (place >= total - SHIFT).astype(jnp.int32)

def reference(features, labels, gain_one, gain_two, w_qkv, w_proj, w_up, w_down, w_head):
    grid = features.reshape(NX, NY, DEPTH, C)
    shifted = jnp.roll(grid, (-SHIFT, -SHIFT, -SHIFT), (0, 1, 2))
    marks = jnp.roll(labels, (-SHIFT, -SHIFT, -SHIFT), (0, 1, 2))
    region = region_ids(NX, NX)[:, None, None] * 9 + region_ids(NY, NY)[None, :, None] * 3 + region_ids(DEPTH, DEPTH)[None, None, :]
    weights = tuple((w.astype(jnp.float32) for w in (w_qkv, w_proj, w_up, w_down, w_head)))
    per = DEPTH // WIN * N_GY

    def split(values):
        return values.reshape((-1, per) + values.shape[1:])
    resid = split(to_windows(shifted.astype(jnp.float32)))
    regions = split(to_windows(region))
    mark_win = split(to_windows(marks))

    def step_fn(carry, piece):
        part_x, part_r, part_m = piece

        def local(values, qkv, proj, up, down, head):
            return block_loss(values, part_r, part_m, gain_one, gain_two, qkv, proj, up, down, head)
        _, pull = jax.vjp(local, part_x, *weights)
        cots = pull(jnp.ones((), jnp.float32))
        return (tuple((a + b for a, b in zip(carry, cots[1:]))), cots[0])
    zeros = tuple((jnp.zeros(w.shape, jnp.float32) for w in weights))
    sums, cot_win = lax.scan(step_fn, zeros, (resid, regions, mark_win))
    cot_grid = from_windows(cot_win.reshape(-1, WIN ** 3, C), NX, NY, DEPTH)
    back = jnp.roll(cot_grid.astype(jnp.bfloat16), (SHIFT, SHIFT, SHIFT), (0, 1, 2))
    scale = 1.0 / math.sqrt(TOKENS)
    return (back.reshape(NX, NY, DEPTH * C), sums[0] * scale, sums[1] * scale, sums[2] * scale, sums[3] * scale, sums[4] * scale)
```

```python
import math

import jax
import jax.numpy as jnp
from jax import lax
from jax.experimental import pallas as pl
from jax.experimental.pallas import tpu as pltpu
from jax.sharding import PartitionSpec as P

BF = jnp.bfloat16
F32 = jnp.float32
C = 48
FF = 192
NH = 3
WIN = 7
SHIFT = 3
DEPTH = 42
WIDTH = DEPTH * C
LAB = 2048
LW = 2176
KP = 352
TL = 384
PT = 343
NZ = 6
NWY = 3
EPS = 1e-5
BIG = 2.0**100
LOG2E_4 = 0.25 * math.log2(math.e)
CH = [(0, 256), (256, 512), (512, 768), (768, 1024), (1024, 1152)]
GC1 = math.sqrt(2 / math.pi)
GC2 = 0.044715 * GC1
MESH = pl.DeviceIdType.MESH


def dot(a,b): return lax.dot_general(a,b,(((1,),(0,)),((),())),preferred_element_type=F32)
def dot_t(a,b): return lax.dot_general(a,b,(((1,),(1,)),((),())),preferred_element_type=F32)
def split3(v):
    a=v.astype(BF); r=v-a.astype(F32); b=r.astype(BF); r=r-b.astype(F32); return a,b,r.astype(BF)
def mean0(v): return jnp.sum(v,axis=0,keepdims=True)*(1.0/C)
def norm(v):
    s=v-mean0(v)
    r=lax.rsqrt(mean0(s*s)+EPS)
    return s*r, r
def norm_back(d,xh,r):
    return (d-mean0(d)-xh*mean0(d*xh))*r

def scratch():
    return dict(
      qkvT=pltpu.VMEM((144,C),BF), projT=pltpu.VMEM((C,C),BF), upT=pltpu.VMEM((FF,C),BF), downT=pltpu.VMEM((C,FF),BF),
      wx=pltpu.VMEM((64,512),BF), kmask=pltpu.VMEM((16,TL),BF), qmask=pltpu.VMEM((16,TL),F32),
      g1=pltpu.VMEM((C,1),F32), g2=pltpu.VMEM((C,1),F32), wd=pltpu.VMEM((C,1),F32),
      a_up=pltpu.VMEM((C,FF),F32), a_down=pltpu.VMEM((C,FF),F32), a_qkv=pltpu.VMEM((C,144),F32), a_proj=pltpu.VMEM((C,C),F32), a_head=pltpu.VMEM((C,128),F32),
    )
def win_scratch():
    return dict(qblk=pltpu.VMEM((160,1152),BF), oblk=pltpu.VMEM((64,1152),BF), P=pltpu.VMEM((KP,1152),BF), D=pltpu.VMEM((KP,1152),BF),
       qt=pltpu.VMEM((1152,C),BF), ot=pltpu.VMEM((1152,C),BF), dkv=pltpu.VMEM((TL,256),BF))

def init(S, Ws, wqkv, wproj, wup, wdown, whead, g1, g2):
    S['qkvT'][...]=wqkv[...].T
    S['projT'][...]=wproj[...].T
    S['upT'][...]=wup[...].T
    S['downT'][...]=wdown[...].T
    wq=wqkv[...].astype(F32)
    wk=wq[:,48:96]; wv=wq[:,96:144]
    z=lambda n: jnp.zeros((C,n),F32)
    top=jnp.concatenate([wk,wk,wk,z(112),wv,z(80),wq[:,0:48],z(80)],axis=1)
    r=lax.broadcasted_iota(jnp.int32,(16,512),0); l=lax.broadcasted_iota(jnp.int32,(16,512),1)
    bot=((l==144+r)|((l>=304)&(l<307)&(r==7))).astype(F32)
    S['wx'][...]=jnp.concatenate([top,bot],axis=0).astype(BF)
    t=lax.broadcasted_iota(jnp.int32,(16,TL),1); r=lax.broadcasted_iota(jnp.int32,(16,TL),0)
    bz=(t>=4*49).astype(F32)
    u=t-49*sum((t>=49*k).astype(jnp.int32) for k in range(1,7))
    bx=(u>=28).astype(F32)
    v=u-7*sum((u>=7*k).astype(jnp.int32) for k in range(1,7))
    by=(v>=4).astype(F32)
    b=jnp.where(r<2,bx,jnp.where(r<4,by,bz))
    first=(r%2)==0
    S['kmask'][...]=jnp.where(r<6,jnp.where(first,1.0-b,b),jnp.where(r==6,(t>=343).astype(F32),(r==7).astype(F32))).astype(BF)
    S['qmask'][...]=jnp.where(r<6,jnp.where(first,b,1.0-b),(r==6).astype(F32))*(-BIG)
    S['g1'][...]=g1[...]; S['g2'][...]=g2[...]
    wh=whead[...].astype(F32)
    S['wd'][...]=wh[:,1:2]-wh[:,0:1]
    for k in ('a_up','a_down','a_qkv','a_proj','a_head'): S[k][...]=jnp.zeros(S[k].shape,F32)
    for w in Ws:
        w['qblk'][...]=jnp.zeros((160,1152),BF)
        w['oblk'][...]=jnp.zeros((64,1152),BF)
        w['dkv'][...]=jnp.zeros((TL,256),BF)

def window(out, x, sign, act, S, W, wqkv, wproj, wup, wdown):
    x=x()
    g1=S['g1'][...]; g2=S['g2'][...]; wd=S['wd'][...]
    xh1,r1=norm(x)
    n1=(xh1*g1).astype(BF)
    yield
    packT=dot(S['qkvT'][...],n1).astype(BF)
    yield
    qT=packT[0:48]; kT=packT[48:96]; vT=packT[96:144]
    tok=dot(jnp.concatenate([n1,S['kmask'][...]],axis=0).T, S['wx'][...]).astype(BF)
    yield
    kaug=tok[:KP,0:160]; vaug=tok[:KP,256:320]; qtok=tok[:,384:432]
    qs=split3(qT.astype(F32)*LOG2E_4)
    r=lax.broadcasted_iota(jnp.int32,(16,1),0)
    sc=jnp.where(r<2,act[0],jnp.where(r<4,act[1],jnp.where(r<6,act[2],1.0)))
    qm=(S['qmask'][...]*sc).astype(BF)
    lane=lax.broadcasted_iota(jnp.int32,(1,C),1)
    for h in range(NH):
        ls=slice(h*TL,(h+1)*TL)
        for i in range(3):
            W['qblk'][48*i+16*h:48*i+16*h+16,ls]=qs[i][16*h:16*h+16]
        W['qblk'][144:160,ls]=qm
        hm=(lane>=16*h)&(lane<16*h+16)
        W['qt'][ls,:]=jnp.where(hm,qtok.astype(F32),0.0).astype(BF)
        yield
    mixp=[]
    vTk=vT[:,:KP]; kTk=kT[:,:KP]
    for a,b in CH:
        p=jnp.exp2(dot(kaug,W['qblk'][:,a:b]))
        yield
        inv=1.0/jnp.sum(p,axis=0,keepdims=True)
        P=(p*inv).astype(BF)
        W['P'][:,a:b]=P
        yield
        mixp.append(dot(vTk,P))
        yield
    mixa=jnp.concatenate(mixp,axis=1)
    mixf=jnp.concatenate([mixa[16*h:16*h+16,h*TL:(h+1)*TL] for h in range(NH)],axis=0)
    mixed=mixf.astype(BF)
    ao=dot(S['projT'][...],mixed).astype(BF).astype(F32)
    yield
    state=(x+ao).astype(BF).astype(F32)
    xh2,r2=norm(state)
    n2=(xh2*g2).astype(BF)
    yield
    hh=dot(S['upT'][...],n2)
    yield
    h2=hh*hh
    t=jnp.tanh(hh*(GC1+GC2*h2))
    s=0.5+0.5*t
    inf=hh*s
    inner=inf.astype(BF)
    dg=s+inf*(1.0-s)*(2*GC1+6*GC2*h2)
    yield
    res=(state+dot(S['downT'][...],inner)).astype(BF).astype(F32)
    yield
    z=jnp.sum(res*wd,axis=0,keepdims=True)
    g=sign*(1.0/(1.0+jnp.exp(-z*sign)))
    yield
    rg=res*g
    S['a_head'][...]+=rg[:,0:128]+rg[:,128:256]+rg[:,256:384]
    dres=(wd*g).astype(BF)
    dinner=dot(wdown[...],dres).astype(BF).astype(F32)
    yield
    S['a_down'][...]+=dot_t(dres,inner)
    yield
    dh=(dinner*dg).astype(BF)
    yield
    S['a_up'][...]+=dot_t(n2,dh)
    yield
    dn2=dot(wup[...],dh).astype(BF).astype(F32)
    yield
    dst=(dres.astype(F32)+norm_back(dn2*g2,xh2,r2)).astype(BF)
    yield
    S['a_proj'][...]+=dot_t(mixed,dst)
    dO=dot(wproj[...],dst).astype(BF)
    yield
    dOf=dO.astype(F32)
    dOtok=dO.T
    yield
    pr=mixf*dOf
    r16=lax.broadcasted_iota(jnp.int32,(16,TL),0)
    for h in range(NH):
        ls=slice(h*TL,(h+1)*TL)
        d=-jnp.sum(pr[16*h:16*h+16],axis=0,keepdims=True)
        d0,d1,d2=split3(d)
        W['oblk'][16*h:16*h+16,ls]=dO[16*h:16*h+16]
        W['oblk'][48:64,ls]=jnp.where(r16==0,d0.astype(F32),jnp.where(r16==1,d1.astype(F32),jnp.where(r16==2,d2.astype(F32),0.0))).astype(BF)
        hm=(lane>=16*h)&(lane<16*h+16)
        W['ot'][ls,:]=jnp.where(hm,dOtok.astype(F32),0.0).astype(BF)
        yield
    dqp=[]
    for a,b in CH:
        ds=W['P'][:,a:b]*dot(vaug,W['oblk'][:,a:b]).astype(BF)
        W['D'][:,a:b]=ds
        yield
        dqp.append(dot(kTk,ds))
        yield
    dqa=jnp.concatenate(dqp,axis=1)
    dq=(0.25*jnp.concatenate([dqa[16*h:16*h+16,h*TL:(h+1)*TL] for h in range(NH)],axis=0)).astype(BF)
    yield
    W['dkv'][0:KP,0:48]=(0.25*dot(W['D'][...],W['qt'][...])).astype(BF)
    yield
    W['dkv'][0:KP,128:176]=dot(W['P'][...],W['ot'][...]).astype(BF)
    yield
    dk=W['dkv'][:,0:128].T[0:48]; dv=W['dkv'][:,128:256].T[0:48]
    yield
    dpack=jnp.concatenate([dq,dk,dv],axis=0)
    S['a_qkv'][...]+=dot_t(n1,dpack)
    yield
    dn1=dot(wqkv[...],dpack).astype(BF).astype(F32)
    yield
    out((dst.astype(F32)+norm_back(dn1*g1,xh1,r1)).astype(BF))


def drive(gens, stagger=0):
    live=[]
    pend=list(gens); k=0
    while pend or live:
        if pend and (k>=stagger or not live):
            live.append(pend.pop(0)); k=0
            if stagger==0:
                live+=pend; pend=[]
        k+=1
        nxt=[]
        for g in live:
            try:
                next(g); nxt.append(g)
            except StopIteration: pass
        live=nxt


S_KEYS = tuple(scratch())
W_KEYS = tuple(win_scratch())


def comm_scratch(nx, ny):
    return dict(
        grid=pltpu.VMEM((WIN, 24, LW), F32),
        rows=pltpu.VMEM((NWY, 64, LW), F32),
        xs=pltpu.VMEM((NWY, 32, LW), BF),
        xr=pltpu.VMEM((NWY, 32, LW), BF),
        ys=pltpu.VMEM((16, LW), BF),
        yr=pltpu.VMEM((16, LW), BF),
        ds=pltpu.VMEM((16, LW), BF),
        dr=pltpu.VMEM((16, LW), BF),
        xwin=pltpu.VMEM((NZ, C, TL), BF),
        sg=pltpu.VMEM((8, TL), F32),
        zt=pltpu.VMEM((LAB, 128), BF),
        back=pltpu.VMEM((NWY, 64, WIDTH), F32),
        bxs=pltpu.VMEM((NWY, 32, WIDTH), BF),
        bxr=pltpu.VMEM((NWY, 32, WIDTH), BF),
        bys=pltpu.VMEM((16, WIDTH), BF),
        byr=pltpu.VMEM((16, WIDTH), BF),
        bds=pltpu.VMEM((16, WIDTH), BF),
        bdr=pltpu.VMEM((16, WIDTH), BF),
        tmp=pltpu.VMEM((64, WIDTH), F32),
        outf=pltpu.VMEM((WIN, 24, WIDTH), F32),
        part=pltpu.VMEM((nx, 256 // nx, 128), F32),
        r1=pltpu.VMEM((nx - 1, 256 // nx, 128), F32),
        csum=pltpu.VMEM((256 // nx, 128), F32),
        r2=pltpu.VMEM((ny - 1, 256 // nx, 128), F32),
        ctot=pltpu.VMEM((256 // nx, 128), F32),
        total=pltpu.VMEM((nx, 256 // nx, 128), F32),
        hs=pltpu.SemaphoreType.DMA((NWY + 2,)),
        hr=pltpu.SemaphoreType.DMA((NWY + 2,)),
        bs=pltpu.SemaphoreType.DMA((NWY + 2,)),
        br=pltpu.SemaphoreType.DMA((NWY + 2,)),
        s1=pltpu.SemaphoreType.DMA((nx - 1,)),
        q1=pltpu.SemaphoreType.DMA((nx - 1,)),
        s2=pltpu.SemaphoreType.DMA((ny - 1,)),
        q2=pltpu.SemaphoreType.DMA((ny - 1,)),
        s3=pltpu.SemaphoreType.DMA((nx - 1,)),
        q3=pltpu.SemaphoreType.DMA((nx - 1,)),
    )


def remote(src, dst, ssem, rsem, to):
    return pltpu.make_async_remote_copy(
        src_ref=src, dst_ref=dst, send_sem=ssem, recv_sem=rsem, device_id=to, device_id_type=MESH
    )


def make_kernel(nx, ny, tokens):
    c_keys = tuple(comm_scratch(nx, ny))

    def kernel(feat, lab, wqkv, wproj, wup, wdown, whead, g1, g2, *refs):
        out, o_qkv, o_proj, o_up, o_down, o_head = refs[:6]
        refs = refs[6:]
        S = dict(zip(S_KEYS, refs))
        refs = refs[len(S_KEYS):]
        Ws = [dict(zip(W_KEYS, refs[i * len(W_KEYS):])) for i in range(NZ)]
        Q = dict(zip(c_keys, refs[NZ * len(W_KEYS):]))
        mx = lax.axis_index("gx")
        my = lax.axis_index("gy")

        def at(dx, dy):
            return (lax.rem(mx + dx + nx, nx), lax.rem(my + dy + ny, ny))

        barrier = pltpu.get_barrier_semaphore()
        peers = [(k, 0) for k in range(1, nx)] + [(0, k) for k in range(1, ny)] + [(1, 1), (-1, -1)]
        for p in peers:
            pl.semaphore_signal(barrier, inc=1, device_id=at(*p), device_id_type=MESH)

        grid = Q["grid"]
        grid[:, 0:21, 0:WIDTH] = feat[...].astype(F32)
        grid[:, 0:21, WIDTH:LAB] = jnp.zeros((WIN, 21, LAB - WIDTH), F32)
        grid[:, 0:21, LAB:LW] = jnp.zeros((WIN, 21, LW - LAB), F32)
        grid[:, 0:21, LAB:LAB + DEPTH] = lab[...].astype(F32)
        tmp = Q["rows"]
        for wy in range(NWY):
            n = WIN if wy < 2 else 4
            for k in range(SHIFT):
                tmp[wy, 7 * k:7 * k + n, :] = grid[k, 7 * wy + 3:7 * wy + 3 + n, :]
            Q["xs"][wy] = tmp[wy, 0:32, :].astype(BF)
        for k in range(4):
            tmp[0, 3 * k:3 * k + 3, :] = grid[3 + k, 0:3, :]
        Q["ys"][...] = tmp[0, 0:16, :].astype(BF)
        for k in range(SHIFT):
            tmp[1, 3 * k:3 * k + 3, :] = grid[k, 0:3, :]
        Q["ds"][...] = tmp[1, 0:16, :].astype(BF)
        pl.semaphore_wait(barrier, len(peers))
        hs, hr = Q["hs"], Q["hr"]
        xcopy = [remote(Q["xs"].at[w], Q["xr"].at[w], hs.at[w], hr.at[w], at(-1, 0)) for w in range(NWY)]
        ycopy = remote(Q["ys"], Q["yr"], hs.at[3], hr.at[3], at(0, -1))
        dcopy = remote(Q["ds"], Q["dr"], hs.at[4], hr.at[4], at(-1, -1))
        xcopy[0].start()
        ycopy.start()
        dcopy.start()
        xcopy[1].start()
        xcopy[2].start()

        init(S, Ws, wqkv, wproj, wup, wdown, whead, g1, g2)
        rows = Q["rows"]
        for wy in range(NWY):
            n = WIN if wy < 2 else 4
            for k in range(4):
                rows[wy, 7 * k:7 * k + n, :] = grid[3 + k, 7 * wy + 3:7 * wy + 3 + n, :]
            rows[wy, 48:64, :] = jnp.zeros((16, LW), F32)
        Q["zt"][...] = jnp.zeros((LAB, 128), BF)

        act_x = (mx == nx - 1).astype(F32)
        last_y = my == ny - 1
        lanes = lax.broadcasted_iota(jnp.int32, (1, TL), 1)

        def step(wy, _):
            remote(Q["xs"].at[wy], Q["xr"].at[wy], hs.at[wy], hr.at[wy], at(-1, 0)).wait()
            rows[wy, 28:49, :] = Q["xr"][wy].astype(F32)[0:21]

            @pl.when(wy == 2)
            def _():
                ycopy.wait()
                dcopy.wait()
                Q["tmp"][0:16, :] = Q["yr"][:, 0:WIDTH].astype(F32)
                Q["tmp"][16:32, :] = Q["dr"][:, 0:WIDTH].astype(F32)
                yl = Q["yr"][:, LAB:LW].astype(F32)
                dl = Q["dr"][:, LAB:LW].astype(F32)
                for k in range(4):
                    rows[2, 7 * k + 4:7 * k + 7, 0:WIDTH] = Q["tmp"][3 * k:3 * k + 3, :]
                    rows[2, 7 * k + 4:7 * k + 7, LAB:LW] = yl[3 * k:3 * k + 3]
                for k in range(SHIFT):
                    rows[2, 28 + 7 * k + 4:28 + 7 * k + 7, 0:WIDTH] = Q["tmp"][16 + 3 * k:16 + 3 * k + 3, :]
                    rows[2, 28 + 7 * k + 4:28 + 7 * k + 7, LAB:LW] = dl[3 * k:3 * k + 3]

            cols = rows[wy].astype(BF).T
            for wz in range(NZ):
                zs = [(7 * wz + j + SHIFT) % DEPTH for j in range(WIN)]
                Q["xwin"][wz] = jnp.concatenate(
                    [cols[C * z:C * z + C, 0:49] for z in zs] + [jnp.zeros((C, TL - PT), BF)], axis=1
                )
                m = jnp.concatenate(
                    [cols[LAB + z:LAB + z + 1, 0:49].astype(F32) for z in zs] + [jnp.zeros((1, TL - PT), F32)],
                    axis=1,
                )
                Q["sg"][wz:wz + 1, :] = jnp.where(lanes < PT, 1.0 - 2.0 * m, 0.0)

            gens = []
            act_y = jnp.logical_and(last_y, wy == 2).astype(F32)
            for wz in range(NZ):
                def put(v, wz=wz):
                    for j in range(WIN):
                        z = (7 * wz + j + SHIFT) % DEPTH
                        Q["zt"][C * z:C * z + C, 0:49] = v[:, 49 * j:49 * j + 49]

                def get(wz=wz):
                    return Q["xwin"][wz].astype(F32)

                act = (act_x, act_y, F32(1.0 if wz == NZ - 1 else 0.0))
                gens.append(window(put, get, Q["sg"][wz:wz + 1, :], act, S, Ws[wz], wqkv, wproj, wup, wdown))
            drive(gens)
            flat = Q["zt"][...].T.astype(F32)[0:64, 0:WIDTH]
            Q["back"][wy] = flat
            Q["bxs"][wy] = jnp.concatenate([flat[28:49], jnp.zeros((11, WIDTH), F32)], axis=0).astype(BF)
            remote(Q["bxs"].at[wy], Q["bxr"].at[wy], Q["bs"].at[wy], Q["br"].at[wy], at(1, 0)).start()
            return 0

        lax.fori_loop(0, NWY, step, 0)

        a_head = jnp.sum(S["a_head"][...], axis=1, keepdims=True)
        acc = jnp.concatenate(
            [S["a_up"][...], S["a_down"][...], S["a_qkv"][...], S["a_proj"][...], a_head, jnp.zeros((C, 63), F32)],
            axis=1,
        )
        part = Q["part"]
        per = 256 // nx
        for j in range(16):
            if j < 15:
                v = acc[16 * (j % 3):16 * (j % 3) + 16, 128 * (j // 3):128 * (j // 3) + 128]
            else:
                v = jnp.zeros((16, 128), F32)
            part[j * 16 // per, (j * 16) % per:(j * 16) % per + 16, :] = v
        first = [
            remote(part.at[lax.rem(mx + k, nx)], Q["r1"].at[k - 1], Q["s1"].at[k - 1], Q["q1"].at[k - 1], at(k, 0))
            for k in range(1, nx)
        ]
        for c in first:
            c.start()

        back, tmp = Q["back"], Q["tmp"]
        for k in range(4):
            tmp[3 * k:3 * k + 3, :] = back[2, 7 * k + 4:7 * k + 7, :]
        for k in range(SHIFT):
            tmp[16 + 3 * k:16 + 3 * k + 3, :] = back[2, 28 + 7 * k + 4:28 + 7 * k + 7, :]
        Q["bys"][...] = tmp[0:16, :].astype(BF)
        Q["bds"][...] = tmp[16:32, :].astype(BF)
        bycopy = remote(Q["bys"], Q["byr"], Q["bs"].at[3], Q["br"].at[3], at(0, 1))
        bdcopy = remote(Q["bds"], Q["bdr"], Q["bs"].at[4], Q["br"].at[4], at(1, 1))
        bycopy.start()
        bdcopy.start()

        for c in first:
            c.wait()
        csum = part[mx]
        for k in range(nx - 1):
            csum = csum + Q["r1"][k]
        Q["csum"][...] = csum
        second = [
            remote(Q["csum"], Q["r2"].at[k - 1], Q["s2"].at[k - 1], Q["q2"].at[k - 1], at(0, k))
            for k in range(1, ny)
        ]
        for c in second:
            c.start()

        outf = Q["outf"]
        for x in range(SHIFT, WIN):
            k = x - SHIFT
            for wy in range(NWY):
                n = WIN if wy < 2 else 4
                outf[x, 7 * wy + 3:7 * wy + 3 + n, :] = back[wy, 7 * k:7 * k + n, :]

        for c in second:
            c.wait()
        order = csum
        for k in range(ny - 1):
            order = order + Q["r2"][k]
        Q["ctot"][...] = order * (1.0 / math.sqrt(tokens))
        Q["total"][mx] = Q["ctot"][...]
        third = [
            remote(Q["ctot"], Q["total"].at[mx], Q["s3"].at[k - 1], Q["q3"].at[k - 1], at(k, 0))
            for k in range(1, nx)
        ]
        for c in third:
            c.start()

        bycopy.wait()
        bdcopy.wait()
        tmp[0:16, :] = Q["byr"][...].astype(F32)
        tmp[16:32, :] = Q["bdr"][...].astype(F32)
        for k in range(4):
            outf[SHIFT + k, 0:3, :] = tmp[3 * k:3 * k + 3, :]
        for k in range(SHIFT):
            outf[k, 0:3, :] = tmp[16 + 3 * k:16 + 3 * k + 3, :]
        for wy in range(NWY):
            remote(Q["bxs"].at[wy], Q["bxr"].at[wy], Q["bs"].at[wy], Q["br"].at[wy], at(1, 0)).wait()
            n = WIN if wy < 2 else 4
            tmp[32:64, :] = Q["bxr"][wy].astype(F32)
            for k in range(SHIFT):
                outf[k, 7 * wy + 3:7 * wy + 3 + n, :] = tmp[32 + 7 * k:32 + 7 * k + n, :]
        out[...] = outf[:, 0:21, :].astype(BF)

        for c in third:
            c.wait()
        total = Q["total"]
        parts = []
        for l in range(5):
            parts.append(
                jnp.concatenate(
                    [total[j * 16 // per, (j * 16) % per:(j * 16) % per + 16, :] for j in range(3 * l, 3 * l + 3)],
                    axis=0,
                )
            )
        whole = jnp.concatenate(parts, axis=1)
        o_up[...] = whole[:, 0:192]
        o_down[...] = whole[:, 192:384]
        o_qkv[...] = whole[:, 384:528]
        o_proj[...] = whole[:, 528:576]
        o_head[...] = whole[:, 576:577]

    return kernel


def body(features, labels, gain_one, gain_two, w_qkv, w_proj, w_up, w_down, w_head):
    nx, ny = lax.axis_size("gx"), lax.axis_size("gy")
    tokens = nx * ny * features.shape[0] * features.shape[1] * DEPTH
    vmem = pl.BlockSpec(memory_space=pltpu.VMEM)
    shapes = [jax.ShapeDtypeStruct(features.shape, BF)] + [
        jax.ShapeDtypeStruct(s, F32) for s in ((C, 144), (C, C), (C, FF), (C, FF), (C, 1))
    ]
    back, d_qkv, d_proj, d_up, d_down, d_head = pl.pallas_call(
        make_kernel(nx, ny, tokens),
        out_shape=shapes,
        in_specs=[vmem] * 9,
        out_specs=[vmem] * 6,
        scratch_shapes=list(scratch().values())
        + list(win_scratch().values()) * NZ
        + list(comm_scratch(nx, ny).values()),
        compiler_params=pltpu.CompilerParams(
            collective_id=0, has_side_effects=True, vmem_limit_bytes=60 * 2**20
        ),
    )(
        features, labels, w_qkv, w_proj, w_up, w_down, w_head,
        gain_one.reshape(C, 1), gain_two.reshape(C, 1),
    )
    return back, d_qkv, d_proj, d_up, d_down.T, jnp.concatenate([-d_head, d_head], axis=1)


def solution(mesh):
    placed = (P("gx", "gy", None), P("gx", "gy", None), P(), P(), P(), P(), P(), P(), P())
    return jax.shard_map(
        body,
        mesh=mesh,
        in_specs=placed,
        out_specs=(P("gx", "gy", None), P(), P(), P(), P(), P()),
        check_vma=False,
    )
```

```python
import math

import jax
import jax.numpy as jnp
from jax import lax
from jax.experimental import pallas as pl
from jax.experimental.pallas import tpu as pltpu
from jax.sharding import PartitionSpec as P

BF = jnp.bfloat16
F32 = jnp.float32
C = 48
FF = 192
NH = 3
WIN = 7
SHIFT = 3
DEPTH = 42
WIDTH = DEPTH * C
LAB = 2048
LW = 2176
KP = 352
TL = 384
PT = 343
NZ = 6
NWY = 3
EPS = 1e-5
BIG = 2.0**100
LOG2E_4 = 0.25 * math.log2(math.e)
CH = [(0, 256), (256, 512), (512, 768), (768, 1024), (1024, 1152)]
GC1 = math.sqrt(2 / math.pi)
GC2 = 0.044715 * GC1
MESH = pl.DeviceIdType.MESH


def dot(a,b): return lax.dot_general(a,b,(((1,),(0,)),((),())),preferred_element_type=F32)
def dot_t(a,b): return lax.dot_general(a,b,(((1,),(1,)),((),())),preferred_element_type=F32)
def split3(v):
    a=v.astype(BF); r=v-a.astype(F32); b=r.astype(BF); r=r-b.astype(F32); return a,b,r.astype(BF)
def mean0(v): return jnp.sum(v,axis=0,keepdims=True)*(1.0/C)
def norm(v):
    s=v-mean0(v)
    r=lax.rsqrt(mean0(s*s)+EPS)
    return s*r, r
def norm_back(d,xh,r):
    return (d-mean0(d)-xh*mean0(d*xh))*r

def scratch():
    return dict(
      qkvT=pltpu.VMEM((144,C),BF), projT=pltpu.VMEM((C,C),BF), upT=pltpu.VMEM((FF,C),BF), downT=pltpu.VMEM((C,FF),BF), down=pltpu.VMEM((FF,C),BF),
      wx=pltpu.VMEM((128,512),BF), kmask=pltpu.VMEM((16,TL),BF), qmask=pltpu.VMEM((16,TL),F32),
      g1=pltpu.VMEM((C,1),F32), g2=pltpu.VMEM((C,1),F32), wd=pltpu.VMEM((C,1),F32),
      a_up=pltpu.VMEM((C,FF),F32), a_down=pltpu.VMEM((C,FF),F32), a_qkv=pltpu.VMEM((C,144),F32), a_proj=pltpu.VMEM((C,C),F32), a_head=pltpu.VMEM((C,128),F32),
    )
def win_scratch():
    return dict(qblk=pltpu.VMEM((240,2304),BF), oblk=pltpu.VMEM((256,2304),BF), P=pltpu.VMEM((KP,2304),BF), D=pltpu.VMEM((KP,2304),BF),
       qt=pltpu.VMEM((2304,128),BF), ot=pltpu.VMEM((2304,128),BF), dkv=pltpu.VMEM((TL,256),BF))

def init(S, Ws, wqkv, wproj, wup, wdownT, whT, g1, g2):
    S['qkvT'][...]=wqkv[...].T
    S['projT'][...]=wproj[...].T
    S['upT'][...]=wup[...].T
    S['downT'][...]=wdownT[...]
    S['down'][...]=wdownT[...].T
    wq=wqkv[...].astype(F32)
    wk=wq[:,48:96]; wv=wq[:,96:144]
    z=lambda n: jnp.zeros((C,n),F32)
    r=lax.broadcasted_iota(jnp.int32,(16,512),0); l=lax.broadcasted_iota(jnp.int32,(16,512),1)
    wqq=wq[:,0:48]
    rows_a=jnp.concatenate([wk,wk,z(160),wv,z(16),wqq,z(144)],axis=1)
    mask_a=((l==96+r)|((l>=304)&(l<307)&(r==7))).astype(F32)
    rows_b=jnp.concatenate([z(128),wk,wk,z(160),wqq,z(16),wv,z(16)],axis=1)
    mask_b=((l==224+r)|((l>=496)&(l<499)&(r==7))).astype(F32)
    S['wx'][...]=jnp.concatenate([rows_a,mask_a,rows_b,mask_b],axis=0).astype(BF)
    t=lax.broadcasted_iota(jnp.int32,(16,TL),1); r=lax.broadcasted_iota(jnp.int32,(16,TL),0)
    bz=(t>=4*49).astype(F32)
    u=t-49*sum((t>=49*k).astype(jnp.int32) for k in range(1,7))
    bx=(u>=28).astype(F32)
    v=u-7*sum((u>=7*k).astype(jnp.int32) for k in range(1,7))
    by=(v>=4).astype(F32)
    b=jnp.where(r<2,bx,jnp.where(r<4,by,bz))
    first=(r%2)==0
    S['kmask'][...]=jnp.where(r<6,jnp.where(first,1.0-b,b),jnp.where(r==6,(t>=343).astype(F32),(r==7).astype(F32))).astype(BF)
    S['qmask'][...]=jnp.where(r<6,jnp.where(first,b,1.0-b),(r==6).astype(F32))*(-BIG)
    wh=whT[...].astype(F32)
    cols=jnp.concatenate([g1[...],g2[...],wh[1:2]-wh[0:1],jnp.zeros((5,C),F32)],axis=0)
    cols=jnp.concatenate([cols,jnp.zeros((8,128-C),F32)],axis=1).T
    S['g1'][...]=cols[0:C,0:1]; S['g2'][...]=cols[0:C,1:2]; S['wd'][...]=cols[0:C,2:3]
    for k in ('a_up','a_down','a_qkv','a_proj','a_head'): S[k][...]=jnp.zeros(S[k].shape,F32)
    for w in Ws:
        w['qblk'][...]=jnp.zeros((240,2304),BF)
        w['oblk'][...]=jnp.zeros((256,2304),BF)
        w['dkv'][...]=jnp.zeros((TL,256),BF)

def split2(v):
    a=v.astype(BF); return a,(v-a.astype(F32)).astype(BF)

def spread(parts):
    def block(j):
        c=j//2; k0=256*c//TL; k=j//3
        return parts[c][16*(k-k0):16*(k-k0)+16,128*(j%2):128*(j%2)+128]
    cols=[jnp.concatenate([block(3*k+i) for i in range(3)],axis=1) for k in range(6)]
    return jnp.concatenate([jnp.concatenate(cols[0:3],axis=0),jnp.concatenate(cols[3:6],axis=0)],axis=1)

def heads_of(c):
    return slice(16*(256*c//TL),16*((256*c+255)//TL)+16)

def window(out, x, sign, act, S, W, wqkv, wproj, wup):
    x=x()
    g1=S['g1'][...]; g2=S['g2'][...]; wd=S['wd'][...]
    n1=(norm(x)[0]*g1).astype(BF)
    yield
    packT=dot(S['qkvT'][...],n1).astype(BF)
    yield
    km=S['kmask'][...]
    tok=dot(jnp.concatenate([n1[:,0:TL],km,n1[:,TL:],km],axis=0).T, S['wx'][...]).astype(BF)
    yield
    qs=split2(packT[0:48].astype(F32)*LOG2E_4)
    r=lax.broadcasted_iota(jnp.int32,(16,1),0)
    lane=lax.broadcasted_iota(jnp.int32,(1,128),1)
    for w in range(2):
        sc=jnp.where(r<2,act[0],jnp.where(r<4,act[1],jnp.where(r<6,act[2+w],1.0)))
        qm=(S['qmask'][...]*sc).astype(BF)
        qtok=tok[:,256+128*w:384+128*w].astype(F32)
        for h in range(NH):
            k=3*w+h; ls=slice(k*TL,(k+1)*TL)
            for i in range(2):
                W['qblk'][128*w+48*i+16*h:128*w+48*i+16*h+16,ls]=qs[i][16*h:16*h+16,TL*w:TL*w+TL]
            W['qblk'][128*w+96:128*w+112,ls]=qm
            l0=64*(1-w)+16*h
            W['qt'][ls,:]=jnp.where((lane>=l0)&(lane<l0+16),qtok,0.0).astype(BF)
            yield
    tk=tok[:KP]
    vT=jnp.concatenate([packT[96:144,0:KP],packT[96:144,TL:TL+KP]],axis=0)
    kT=jnp.concatenate([packT[48:96,0:KP],packT[48:96,TL:TL+KP]],axis=0)
    def fwd_dot(c):
        rs=slice(0,112) if c<4 else (slice(0,240) if c==4 else slice(128,240))
        return jnp.exp2(dot(tk[:,rs],W['qblk'][rs,256*c:256*c+256]))
    mixp=[]
    p=fwd_dot(0)
    for c in range(9):
        yield
        nxt=fwd_dot(c+1) if c<8 else None
        P=(p*(1.0/jnp.sum(p,axis=0,keepdims=True))).astype(BF)
        W['P'][:,256*c:256*c+256]=P
        yield
        mixp.append(dot(vT[heads_of(c)],P))
        p=nxt
    mixf=spread(mixp)
    mixed=mixf.astype(BF)
    ao=dot(S['projT'][...],mixed).astype(BF).astype(F32)
    yield
    state=(x+ao).astype(BF).astype(F32)
    xh2,r2=norm(state)
    n2=(xh2*g2).astype(BF)
    yield
    hh=dot(S['upT'][...],n2)
    yield
    h2=hh*hh
    t=jnp.tanh(hh*(GC1+GC2*h2))
    s=0.5+0.5*t
    inf=hh*s
    inner=inf.astype(BF)
    dg=s+inf*(1.0-s)*(2*GC1+6*GC2*h2)
    yield
    res=(state+dot(S['downT'][...],inner)).astype(BF).astype(F32)
    yield
    z=jnp.sum(res*wd,axis=0,keepdims=True)
    g=sign*(1.0/(1.0+jnp.exp(-z*sign)))
    rg=res*g
    S['a_head'][...]+=sum(rg[:,128*i:128*i+128] for i in range(1,6))+rg[:,0:128]
    dres=(wd*g).astype(BF)
    yield
    dinner=dot(S['down'][...],dres).astype(BF).astype(F32)
    yield
    S['a_down'][...]+=dot_t(dres,inner)
    yield
    dh=(dinner*dg).astype(BF)
    yield
    S['a_up'][...]+=dot_t(n2,dh)
    yield
    dn2=dot(wup[...],dh).astype(BF).astype(F32)
    yield
    dst=(dres.astype(F32)+norm_back(dn2*g2,xh2,r2)).astype(BF)
    yield
    S['a_proj'][...]+=dot_t(mixed,dst)
    yield
    dO=dot(wproj[...],dst).astype(BF)
    yield
    zr=jnp.zeros((16,TL),BF)
    dOtok=jnp.concatenate([dO[:,TL:],zr,dO[:,0:TL],zr],axis=0).T.astype(F32)
    yield
    pr=mixf*dO.astype(F32)
    r16=lax.broadcasted_iota(jnp.int32,(16,TL),0)
    for w in range(2):
        for h in range(NH):
            k=3*w+h; ls=slice(k*TL,(k+1)*TL); ws=slice(TL*w,TL*w+TL); o=192*w
            d0,d1,d2=split3(-jnp.sum(pr[16*h:16*h+16,ws],axis=0,keepdims=True))
            W['oblk'][o+16*h:o+16*h+16,ls]=dO[16*h:16*h+16,ws]
            W['oblk'][o+48:o+64,ls]=jnp.where(r16==0,d0.astype(F32),jnp.where(r16==1,d1.astype(F32),jnp.where(r16==2,d2.astype(F32),0.0))).astype(BF)
            l0=64*(1-w)+16*h
            W['ot'][ls,:]=jnp.where((lane>=l0)&(lane<l0+16),dOtok,0.0).astype(BF)
            yield
    def bwd_dot(c):
        rs=slice(0,64) if c<4 else (slice(0,256) if c==4 else slice(128,256))
        return dot(tk[:,rs.start+256:rs.stop+256],W['oblk'][rs,256*c:256*c+256]).astype(BF)
    dqp=[]
    dp=bwd_dot(0)
    for c in range(9):
        yield
        nxt=bwd_dot(c+1) if c<8 else None
        cs=slice(256*c,256*c+256)
        ds=W['P'][:,cs]*dp
        W['D'][:,cs]=ds
        yield
        dqp.append(dot(kT[heads_of(c)],ds))
        dp=nxt
    dq=(0.25*spread(dqp)).astype(BF)
    yield
    W['dkv'][0:KP,128:256]=dot(W['P'][...],W['ot'][...]).astype(BF)
    yield
    W['dkv'][0:KP,0:128]=(0.25*dot(W['D'][...],W['qt'][...])).astype(BF)
    yield
    dk=W['dkv'][:,0:128].T; dv=W['dkv'][:,128:256].T
    dpack=jnp.concatenate([dq,jnp.concatenate([dk[64:112],dk[0:48]],axis=1),jnp.concatenate([dv[64:112],dv[0:48]],axis=1)],axis=0)
    yield
    S['a_qkv'][...]+=dot_t(n1,dpack)
    out(dpack,dst)

def finish(x, dpack, dst, S, wqkv):
    g1=S['g1'][...]
    xh1,r1=norm(x)
    dn1=dot(wqkv[...],dpack).astype(BF).astype(F32)
    return (dst.astype(F32)+norm_back(dn1*g1,xh1,r1)).astype(BF)


def drive(gens, stagger=0):
    live=[]
    pend=list(gens); k=0
    while pend or live:
        if pend and (k>=stagger or not live):
            live.append(pend.pop(0)); k=0
            if stagger==0:
                live+=pend; pend=[]
        k+=1
        nxt=[]
        for g in live:
            try:
                next(g); nxt.append(g)
            except StopIteration: pass
        live=nxt


G1 = 8
G2 = 16
ROWS = 32
NP = 3
S_KEYS = tuple(scratch())
W_KEYS = tuple(win_scratch())


def comm_scratch(nx, ny):
    return dict(
        grid=pltpu.VMEM((WIN, 24, LW), F32),
        rows=pltpu.VMEM((NWY, 64, LW), F32),
        xs=pltpu.VMEM((NWY, 32, LW), BF),
        xr=pltpu.VMEM((NWY, 32, LW), BF),
        ys=pltpu.VMEM((16, LW), BF),
        yr=pltpu.VMEM((16, LW), BF),
        ds=pltpu.VMEM((16, LW), BF),
        dr=pltpu.VMEM((16, LW), BF),
        xwin=pltpu.VMEM((NWY * NP, C, 2 * TL), BF),
        dpk=pltpu.VMEM((NWY * NP, 3 * C, 2 * TL), BF),
        dst=pltpu.VMEM((NWY * NP, C, 2 * TL), BF),
        sg=pltpu.VMEM((8, 2 * TL), F32),
        zt=pltpu.VMEM((LAB, 128), BF),
        back=pltpu.VMEM((NWY, 64, WIDTH), F32),
        bxs=pltpu.VMEM((NWY, 32, WIDTH), BF),
        bxr=pltpu.VMEM((NWY, 32, WIDTH), BF),
        bys=pltpu.VMEM((16, WIDTH), BF),
        byr=pltpu.VMEM((16, WIDTH), BF),
        bds=pltpu.VMEM((16, WIDTH), BF),
        bdr=pltpu.VMEM((16, WIDTH), BF),
        tmp=pltpu.VMEM((64, WIDTH), F32),
        outf=pltpu.VMEM((WIN, 24, WIDTH), F32),
        part=pltpu.VMEM((G1, ROWS, 128), F32),
        r1=pltpu.VMEM((G1 - 1, ROWS, 128), F32),
        r2=pltpu.VMEM((G2, ROWS, 128), BF),
        total=pltpu.VMEM((G1, ROWS, 128), F32),
        hs=pltpu.SemaphoreType.DMA((NWY + 2,)),
        hr=pltpu.SemaphoreType.DMA((NWY + 2,)),
        bs=pltpu.SemaphoreType.DMA((NWY + 2,)),
        br=pltpu.SemaphoreType.DMA((NWY + 2,)),
        s1=pltpu.SemaphoreType.DMA((G1 - 1,)),
        q1=pltpu.SemaphoreType.DMA((G1 - 1,)),
        s2=pltpu.SemaphoreType.DMA((G2 - 1,)),
        q2=pltpu.SemaphoreType.DMA((G2 - 1,)),
        s3=pltpu.SemaphoreType.DMA((G1 - 1,)),
        q3=pltpu.SemaphoreType.DMA((G1 - 1,)),
    )


def remote(src, dst, ssem, rsem, to):
    return pltpu.make_async_remote_copy(
        src_ref=src, dst_ref=dst, send_sem=ssem, recv_sem=rsem, device_id=to, device_id_type=MESH
    )


def make_kernel(nx, ny, tokens):
    c_keys = tuple(comm_scratch(nx, ny))

    def kernel(feat, lab, wqkv, wproj, wup, wdown, whead, g1, g2, *refs):
        out, o_sum = refs[:2]
        refs = refs[2:]
        S = dict(zip(S_KEYS, refs))
        refs = refs[len(S_KEYS):]
        Ws = [dict(zip(W_KEYS, refs[i * len(W_KEYS):])) for i in range(NP)]
        Q = dict(zip(c_keys, refs[NP * len(W_KEYS):]))
        mx = lax.axis_index("gx")
        my = lax.axis_index("gy")

        def at(dx, dy):
            return (lax.rem(mx + dx + nx, nx), lax.rem(my + dy + ny, ny))

        half = lax.rem(lax.div(mx, 2), 2)
        core = lax.rem(mx, 2)
        px = lax.div(mx, 4)
        m1 = px * 2 + core
        m2 = half * ny + my

        def in_one(k):
            x2 = lax.rem(px + k // 2, 4)
            c2 = lax.rem(core + k % 2, 2)
            return x2 * 2 + c2, ((x2 * 2 + half) * 2 + c2, my)

        def in_two(k):
            h2 = lax.rem(half + k // ny, 2)
            return ((px * 2 + h2) * 2 + core, lax.rem(my + k % ny, ny))

        barrier = pltpu.get_barrier_semaphore()
        peers = [at(1, 0), at(-1, 0), at(1, 1), at(-1, -1)]
        peers += [in_one(k)[1] for k in range(1, G1)] + [in_two(k) for k in range(1, G2)]
        for p in peers:
            pl.semaphore_signal(barrier, inc=1, device_id=p, device_id_type=MESH)

        grid = Q["grid"]
        grid[:, 0:21, 0:WIDTH] = feat[...].astype(F32)
        grid[:, 0:21, WIDTH:LAB] = jnp.zeros((WIN, 21, LAB - WIDTH), F32)
        grid[:, 0:21, LAB:LW] = jnp.zeros((WIN, 21, LW - LAB), F32)
        grid[:, 0:21, LAB:LAB + DEPTH] = lab[...].astype(F32)
        tmp = Q["rows"]
        for wy in range(NWY):
            n = WIN if wy < 2 else 4
            for k in range(SHIFT):
                tmp[wy, 7 * k:7 * k + n, :] = grid[k, 7 * wy + 3:7 * wy + 3 + n, :]
            Q["xs"][wy] = tmp[wy, 0:32, :].astype(BF)
        for k in range(4):
            tmp[0, 3 * k:3 * k + 3, :] = grid[3 + k, 0:3, :]
        Q["ys"][...] = tmp[0, 0:16, :].astype(BF)
        for k in range(SHIFT):
            tmp[1, 3 * k:3 * k + 3, :] = grid[k, 0:3, :]
        Q["ds"][...] = tmp[1, 0:16, :].astype(BF)
        pl.semaphore_wait(barrier, len(peers))
        hs, hr = Q["hs"], Q["hr"]
        xcopy = [remote(Q["xs"].at[w], Q["xr"].at[w], hs.at[w], hr.at[w], at(-1, 0)) for w in range(NWY)]
        ycopy = remote(Q["ys"], Q["yr"], hs.at[3], hr.at[3], at(0, -1))
        dcopy = remote(Q["ds"], Q["dr"], hs.at[4], hr.at[4], at(-1, -1))
        xcopy[0].start()
        ycopy.start()
        dcopy.start()
        xcopy[1].start()
        xcopy[2].start()

        init(S, Ws, wqkv, wproj, wup, wdown, whead, g1, g2)
        rows = Q["rows"]
        for wy in range(NWY):
            n = WIN if wy < 2 else 4
            for k in range(4):
                rows[wy, 7 * k:7 * k + n, :] = grid[3 + k, 7 * wy + 3:7 * wy + 3 + n, :]
            rows[wy, 48:64, :] = jnp.zeros((16, LW), F32)
        Q["zt"][...] = jnp.zeros((LAB, 128), BF)

        act_x = (mx == nx - 1).astype(F32)
        last_y = my == ny - 1
        lanes = lax.broadcasted_iota(jnp.int32, (1, TL), 1)

        def step(wy, _):
            remote(Q["xs"].at[wy], Q["xr"].at[wy], hs.at[wy], hr.at[wy], at(-1, 0)).wait()
            rows[wy, 28:49, :] = Q["xr"][wy].astype(F32)[0:21]

            @pl.when(wy == 2)
            def _():
                ycopy.wait()
                dcopy.wait()
                Q["tmp"][0:16, :] = Q["yr"][:, 0:WIDTH].astype(F32)
                Q["tmp"][16:32, :] = Q["dr"][:, 0:WIDTH].astype(F32)
                yl = Q["yr"][:, LAB:LW].astype(F32)
                dl = Q["dr"][:, LAB:LW].astype(F32)
                for k in range(4):
                    rows[2, 7 * k + 4:7 * k + 7, 0:WIDTH] = Q["tmp"][3 * k:3 * k + 3, :]
                    rows[2, 7 * k + 4:7 * k + 7, LAB:LW] = yl[3 * k:3 * k + 3]
                for k in range(SHIFT):
                    rows[2, 28 + 7 * k + 4:28 + 7 * k + 7, 0:WIDTH] = Q["tmp"][16 + 3 * k:16 + 3 * k + 3, :]
                    rows[2, 28 + 7 * k + 4:28 + 7 * k + 7, LAB:LW] = dl[3 * k:3 * k + 3]

            cols = rows[wy].astype(BF).T
            zero = jnp.zeros((C, TL - PT), BF)
            zrow = jnp.zeros((1, TL - PT), F32)
            for p in range(NP):
                zs = [[(7 * wz + j + SHIFT) % DEPTH for j in range(WIN)] for wz in (2 * p, 2 * p + 1)]
                halves = [jnp.concatenate([cols[C * z:C * z + C, 0:49] for z in w] + [zero], axis=1) for w in zs]
                Q["xwin"][NP * wy + p] = jnp.concatenate(halves, axis=1)
                marks = [
                    jnp.concatenate([cols[LAB + z:LAB + z + 1, 0:49].astype(F32) for z in w] + [zrow], axis=1)
                    for w in zs
                ]
                Q["sg"][p:p + 1, :] = jnp.concatenate(
                    [jnp.where(lanes < PT, 1.0 - 2.0 * m, 0.0) for m in marks], axis=1
                )

            gens = []
            act_y = jnp.logical_and(last_y, wy == 2).astype(F32)
            for p in range(NP):
                def put(dpack, dst, p=p):
                    Q["dpk"][NP * wy + p] = dpack
                    Q["dst"][NP * wy + p] = dst

                def get(p=p):
                    return Q["xwin"][NP * wy + p].astype(F32)

                act = (act_x, act_y, F32(0.0), F32(1.0 if p == NP - 1 else 0.0))
                gens.append(window(put, get, Q["sg"][p:p + 1, :], act, S, Ws[p], wqkv, wproj, wup))
            drive(gens, 1)
            return 0

        lax.fori_loop(0, NWY, step, 0)

        a_head = jnp.sum(S["a_head"][...], axis=1, keepdims=True)
        acc = jnp.concatenate(
            [S["a_up"][...], S["a_down"][...], S["a_qkv"][...], S["a_proj"][...], a_head, jnp.zeros((C, 63), F32)],
            axis=1,
        )
        part = Q["part"]
        for j in range(16):
            if j < 15:
                v = acc[16 * (j % 3):16 * (j % 3) + 16, 128 * (j // 3):128 * (j // 3) + 128]
            else:
                v = jnp.zeros((16, 128), F32)
            part[j // 2, 16 * (j % 2):16 * (j % 2) + 16, :] = v
        first = []
        for k in range(1, G1):
            slot, to = in_one(k)
            first.append(remote(part.at[slot], Q["r1"].at[k - 1], Q["s1"].at[k - 1], Q["q1"].at[k - 1], to))
        for c in first:
            c.start()

        def tail(wy):
            for p in range(NP):
                v = finish(Q["xwin"][NP * wy + p].astype(F32), Q["dpk"][NP * wy + p], Q["dst"][NP * wy + p], S, wqkv)
                for i in range(2):
                    for j in range(WIN):
                        z = (7 * (2 * p + i) + j + SHIFT) % DEPTH
                        Q["zt"][C * z:C * z + C, 0:49] = v[:, TL * i + 49 * j:TL * i + 49 * j + 49]
            flat = Q["zt"][...].T.astype(F32)[0:64, 0:WIDTH]
            Q["back"][wy] = flat
            Q["bxs"][wy] = jnp.concatenate([flat[28:49], jnp.zeros((11, WIDTH), F32)], axis=0).astype(BF)
            remote(Q["bxs"].at[wy], Q["bxr"].at[wy], Q["bs"].at[wy], Q["br"].at[wy], at(1, 0)).start()

        tail(2)
        back, tmp = Q["back"], Q["tmp"]
        for k in range(4):
            tmp[3 * k:3 * k + 3, :] = back[2, 7 * k + 4:7 * k + 7, :]
        for k in range(SHIFT):
            tmp[16 + 3 * k:16 + 3 * k + 3, :] = back[2, 28 + 7 * k + 4:28 + 7 * k + 7, :]
        Q["bys"][...] = tmp[0:16, :].astype(BF)
        Q["bds"][...] = tmp[16:32, :].astype(BF)
        bycopy = remote(Q["bys"], Q["byr"], Q["bs"].at[3], Q["br"].at[3], at(0, 1))
        bdcopy = remote(Q["bds"], Q["bdr"], Q["bs"].at[4], Q["br"].at[4], at(1, 1))
        bycopy.start()
        bdcopy.start()

        for c in first:
            c.wait()
        csum = part[m1]
        for k in range(G1 - 1):
            csum = csum + Q["r1"][k]
        r2 = Q["r2"]
        r2[m2] = csum.astype(BF)
        second = [
            remote(r2.at[m2], r2.at[m2], Q["s2"].at[k - 1], Q["q2"].at[k - 1], in_two(k)) for k in range(1, G2)
        ]
        for c in second:
            c.start()

        tail(0)
        tail(1)

        outf = Q["outf"]
        for x in range(SHIFT, WIN):
            k = x - SHIFT
            for wy in range(NWY):
                n = WIN if wy < 2 else 4
                outf[x, 7 * wy + 3:7 * wy + 3 + n, :] = back[wy, 7 * k:7 * k + n, :]

        for c in second:
            c.wait()
        ctot = r2[0].astype(F32)
        for k in range(1, G2):
            ctot = ctot + r2[k].astype(F32)
        total = Q["total"]
        total[m1] = ctot * (1.0 / math.sqrt(tokens))
        third = [
            remote(total.at[m1], total.at[m1], Q["s3"].at[k - 1], Q["q3"].at[k - 1], in_one(k)[1])
            for k in range(1, G1)
        ]
        for c in third:
            c.start()

        bycopy.wait()
        bdcopy.wait()
        tmp[0:16, :] = Q["byr"][...].astype(F32)
        tmp[16:32, :] = Q["bdr"][...].astype(F32)
        for k in range(4):
            outf[SHIFT + k, 0:3, :] = tmp[3 * k:3 * k + 3, :]
        for k in range(SHIFT):
            outf[k, 0:3, :] = tmp[16 + 3 * k:16 + 3 * k + 3, :]
        for wy in range(NWY):
            remote(Q["bxs"].at[wy], Q["bxr"].at[wy], Q["bs"].at[wy], Q["br"].at[wy], at(1, 0)).wait()
            n = WIN if wy < 2 else 4
            tmp[32:64, :] = Q["bxr"][wy].astype(F32)
            for k in range(SHIFT):
                outf[k, 7 * wy + 3:7 * wy + 3 + n, :] = tmp[32 + 7 * k:32 + 7 * k + n, :]
        out[...] = outf[:, 0:21, :].astype(BF)

        for c in third:
            c.wait()
        parts = []
        for l in range(5):
            parts.append(
                jnp.concatenate(
                    [total[j // 2, 16 * (j % 2):16 * (j % 2) + 16, :] for j in range(3 * l, 3 * l + 3)], axis=0
                )
            )
        whole = jnp.concatenate(parts, axis=1)
        o_sum[...] = whole

    return kernel


def deliver(back, sums, out, o_qkv, o_proj, o_up, o_down, o_head):
    out[...] = back[...]
    o_up[...] = sums[:, 0:192]
    o_down[...] = sums[:, 192:384]
    o_qkv[...] = sums[:, 384:528]
    o_proj[...] = sums[:, 528:576]
    col = sums[:, 512:640].T[64:65]
    o_head[...] = jnp.concatenate([-col, col], axis=0)


def body(features, labels, gain_one, gain_two, w_qkv, w_proj, w_up, w_down, w_head):
    nx, ny = lax.axis_size("gx"), lax.axis_size("gy")
    tokens = nx * ny * features.shape[0] * features.shape[1] * DEPTH
    vmem = pl.BlockSpec(memory_space=pltpu.VMEM)
    back, sums = pl.pallas_call(
        make_kernel(nx, ny, tokens),
        out_shape=[jax.ShapeDtypeStruct(features.shape, BF), jax.ShapeDtypeStruct((C, 640), F32)],
        in_specs=[vmem] * 9,
        out_specs=[vmem] * 2,
        scratch_shapes=list(scratch().values())
        + list(win_scratch().values()) * NP
        + list(comm_scratch(nx, ny).values()),
        compiler_params=pltpu.CompilerParams(
            collective_id=0, has_side_effects=True, vmem_limit_bytes=60 * 2**20
        ),
    )(
        features, labels, w_qkv, w_proj, w_up, w_down.T, w_head.T,
        gain_one.reshape(1, C), gain_two.reshape(1, C),
    )
    out, d_qkv, d_proj, d_up, d_down, d_head = pl.pallas_call(
        deliver,
        out_shape=[jax.ShapeDtypeStruct(features.shape, BF)] + [
            jax.ShapeDtypeStruct(s, F32) for s in ((C, 144), (C, C), (C, FF), (C, FF), (2, C))
        ],
        in_specs=[vmem] * 2,
        out_specs=[vmem] * 6,
    )(back, sums)
    return out, d_qkv, d_proj, d_up, d_down.T, d_head.T


def solution(mesh):
    placed = (P("gx", "gy", None), P("gx", "gy", None), P(), P(), P(), P(), P(), P(), P())
    return jax.shard_map(
        body,
        mesh=mesh,
        in_specs=placed,
        out_specs=(P("gx", "gy", None), P(), P(), P(), P(), P()),
        check_vma=False,
    )
```

```python
import math

import jax
import jax.numpy as jnp
from jax import lax
from jax.experimental import pallas as pl
from jax.experimental.pallas import tpu as pltpu
from jax.sharding import PartitionSpec as P

BF = jnp.bfloat16
F32 = jnp.float32
C = 48
FF = 192
NH = 3
WIN = 7
SHIFT = 3
DEPTH = 42
WIDTH = DEPTH * C
LAB = 2048
LW = 2176
KP = 352
TL = 384
PT = 343
NZ = 6
NWY = 3
EPS = 1e-5
BIG = 2.0**100
LOG2E_4 = 0.25 * math.log2(math.e)
CH = [(0, 256), (256, 512), (512, 768), (768, 1024), (1024, 1152)]
GC1 = math.sqrt(2 / math.pi)
GC2 = 0.044715 * GC1
MESH = pl.DeviceIdType.MESH


def dot(a,b): return lax.dot_general(a,b,(((1,),(0,)),((),())),preferred_element_type=F32)
def dot_t(a,b): return lax.dot_general(a,b,(((1,),(1,)),((),())),preferred_element_type=F32)
def split3(v):
    a=v.astype(BF); r=v-a.astype(F32); b=r.astype(BF); r=r-b.astype(F32); return a,b,r.astype(BF)
def mean0(v): return jnp.sum(v,axis=0,keepdims=True)*(1.0/C)
def norm(v):
    s=v-mean0(v)
    r=lax.rsqrt(mean0(s*s)+EPS)
    return s*r, r
def norm_back(d,xh,r):
    return (d-mean0(d)-xh*mean0(d*xh))*r

def scratch():
    return dict(
      qkvT=pltpu.VMEM((144,C),BF), projT=pltpu.VMEM((C,C),BF), upT=pltpu.VMEM((FF,C),BF), downT=pltpu.VMEM((C,FF),BF), down=pltpu.VMEM((FF,C),BF),
      wx=pltpu.VMEM((128,512),BF), kmask=pltpu.VMEM((16,TL),BF), qmask=pltpu.VMEM((16,TL),F32),
      g1=pltpu.VMEM((C,1),F32), g2=pltpu.VMEM((C,1),F32), wd=pltpu.VMEM((C,1),F32),
      a_up=pltpu.VMEM((C,FF),F32), a_down=pltpu.VMEM((C,FF),F32), a_qkv=pltpu.VMEM((C,144),F32), a_proj=pltpu.VMEM((C,C),F32), a_head=pltpu.VMEM((C,128),F32),
    )
def win_scratch():
    return dict(oblk=pltpu.VMEM((256,2304),BF), P=pltpu.VMEM((KP,2304),BF),
       qt=pltpu.VMEM((2304,128),BF), ot=pltpu.VMEM((2304,128),BF), tokv=pltpu.VMEM((TL,256),BF), kT=pltpu.VMEM((96,TL),BF), n1=pltpu.VMEM((C,2*TL),BF))

def tmp_scratch():
    return dict(qblk=pltpu.VMEM((240,2304),BF), D=pltpu.VMEM((KP,2304),BF), dkv=pltpu.VMEM((TL,256),BF))

def init(S, Ws, Ts, wqkv, wproj, wup, wdownT, whT, g1, g2):
    S['qkvT'][...]=wqkv[...].T
    S['projT'][...]=wproj[...].T
    S['upT'][...]=wup[...].T
    S['downT'][...]=wdownT[...]
    S['down'][...]=wdownT[...].T
    wq=wqkv[...].astype(F32)
    wk=wq[:,48:96]; wv=wq[:,96:144]
    z=lambda n: jnp.zeros((C,n),F32)
    r=lax.broadcasted_iota(jnp.int32,(16,512),0); l=lax.broadcasted_iota(jnp.int32,(16,512),1)
    wqq=wq[:,0:48]
    rows_a=jnp.concatenate([wk,wk,z(160),wv,z(16),wqq,z(144)],axis=1)
    mask_a=((l==96+r)|((l>=304)&(l<307)&(r==7))).astype(F32)
    rows_b=jnp.concatenate([z(128),wk,wk,z(160),wqq,z(16),wv,z(16)],axis=1)
    mask_b=((l==224+r)|((l>=496)&(l<499)&(r==7))).astype(F32)
    S['wx'][...]=jnp.concatenate([rows_a,mask_a,rows_b,mask_b],axis=0).astype(BF)
    t=lax.broadcasted_iota(jnp.int32,(16,TL),1); r=lax.broadcasted_iota(jnp.int32,(16,TL),0)
    bz=(t>=4*49).astype(F32)
    u=t-49*sum((t>=49*k).astype(jnp.int32) for k in range(1,7))
    bx=(u>=28).astype(F32)
    v=u-7*sum((u>=7*k).astype(jnp.int32) for k in range(1,7))
    by=(v>=4).astype(F32)
    b=jnp.where(r<2,bx,jnp.where(r<4,by,bz))
    first=(r%2)==0
    S['kmask'][...]=jnp.where(r<6,jnp.where(first,1.0-b,b),jnp.where(r==6,(t>=343).astype(F32),(r==7).astype(F32))).astype(BF)
    S['qmask'][...]=jnp.where(r<6,jnp.where(first,b,1.0-b),(r==6).astype(F32))*(-BIG)
    wh=whT[...].astype(F32)
    cols=jnp.concatenate([g1[...],g2[...],wh[1:2]-wh[0:1],jnp.zeros((5,C),F32)],axis=0)
    cols=jnp.concatenate([cols,jnp.zeros((8,128-C),F32)],axis=1).T
    S['g1'][...]=cols[0:C,0:1]; S['g2'][...]=cols[0:C,1:2]; S['wd'][...]=cols[0:C,2:3]
    for k in ('a_up','a_down','a_qkv','a_proj','a_head'): S[k][...]=jnp.zeros(S[k].shape,F32)
    for w in Ws:
        w['oblk'][...]=jnp.zeros((256,2304),BF)
    for t in Ts:
        t['qblk'][...]=jnp.zeros((240,2304),BF)
        t['dkv'][...]=jnp.zeros((TL,256),BF)

def lane_mask(l0):
    lane=lax.broadcasted_iota(jnp.int32,(1,128),1)
    return jnp.where((lane>=l0)&(lane<l0+16),1.0,0.0).astype(BF)

def split2(v):
    a=v.astype(BF); return a,(v-a.astype(F32)).astype(BF)

def spread(parts):
    def block(j):
        c=j//2; k0=256*c//TL; k=j//3
        return parts[c][16*(k-k0):16*(k-k0)+16,128*(j%2):128*(j%2)+128]
    cols=[jnp.concatenate([block(3*k+i) for i in range(3)],axis=1) for k in range(6)]
    return jnp.concatenate([jnp.concatenate(cols[0:3],axis=0),jnp.concatenate(cols[3:6],axis=0)],axis=1)

def heads_of(c):
    return slice(16*(256*c//TL),16*((256*c+255)//TL)+16)

def window(out, x, sign, act, S, W, T, wproj, wup):
    x=x()
    g1=S['g1'][...]; g2=S['g2'][...]; wd=S['wd'][...]
    n1=(norm(x)[0]*g1).astype(BF)
    yield
    packT=dot(S['qkvT'][...],n1).astype(BF)
    yield
    km=S['kmask'][...]
    tok=dot(jnp.concatenate([n1[:,0:TL],km,n1[:,TL:],km],axis=0).T, S['wx'][...]).astype(BF)
    yield
    qs=split2(packT[0:48].astype(F32)*LOG2E_4)
    r=lax.broadcasted_iota(jnp.int32,(16,1),0)
    W['n1'][...]=n1
    W['tokv'][...]=tok[:,256:512]
    for w in range(2):
        W['kT'][48*w:48*w+48,:]=packT[48:96,TL*w:TL*w+TL]
    yield
    for w in range(2):
        sc=jnp.where(r<2,act[0],jnp.where(r<4,act[1],jnp.where(r<6,act[2+w],1.0)))
        qm=(S['qmask'][...]*sc).astype(BF)
        qtok=tok[:,256+128*w:384+128*w]
        for h in range(NH):
            k=3*w+h; ls=slice(k*TL,(k+1)*TL)
            for i in range(2):
                T['qblk'][128*w+48*i+16*h:128*w+48*i+16*h+16,ls]=qs[i][16*h:16*h+16,TL*w:TL*w+TL]
            T['qblk'][128*w+96:128*w+112,ls]=qm
            l0=64*(1-w)+16*h
            W['qt'][ls,:]=qtok*lane_mask(l0)
            yield
    tk=tok[:KP]
    vT=jnp.concatenate([packT[96:144,0:KP],packT[96:144,TL:TL+KP]],axis=0)
    def fwd_dot(c):
        rs=slice(0,112) if c<4 else (slice(0,240) if c==4 else slice(128,240))
        return jnp.exp2(dot(tk[:,rs],T['qblk'][rs,256*c:256*c+256]))
    mixp=[]
    p=fwd_dot(0)
    for c in range(9):
        yield
        nxt=fwd_dot(c+1) if c<8 else None
        P=(p*(1.0/jnp.sum(p,axis=0,keepdims=True))).astype(BF)
        W['P'][:,256*c:256*c+256]=P
        yield
        mixp.append(dot(vT[heads_of(c)],P))
        p=nxt
    mixf=spread(mixp)
    mixed=mixf.astype(BF)
    ao=dot(S['projT'][...],mixed).astype(BF).astype(F32)
    yield
    state=(x+ao).astype(BF).astype(F32)
    xh2,r2=norm(state)
    n2=(xh2*g2).astype(BF)
    yield
    hh=dot(S['upT'][...],n2)
    yield
    h2=hh*hh
    t=jnp.tanh(hh*(GC1+GC2*h2))
    s=0.5+0.5*t
    inf=hh*s
    inner=inf.astype(BF)
    dg=s+inf*(1.0-s)*(2*GC1+6*GC2*h2)
    yield
    res=(state+dot(S['downT'][...],inner)).astype(BF).astype(F32)
    yield
    z=jnp.sum(res*wd,axis=0,keepdims=True)
    g=sign*(1.0/(1.0+jnp.exp(-z*sign)))
    rg=res*g
    S['a_head'][...]+=sum(rg[:,128*i:128*i+128] for i in range(1,6))+rg[:,0:128]
    dres=(wd*g).astype(BF)
    yield
    dinner=dot(S['down'][...],dres).astype(BF).astype(F32)
    yield
    S['a_down'][...]+=dot_t(dres,inner)
    yield
    dh=(dinner*dg).astype(BF)
    yield
    S['a_up'][...]+=dot_t(n2,dh)
    yield
    dn2=dot(wup[...],dh).astype(BF).astype(F32)
    yield
    dst=(dres.astype(F32)+norm_back(dn2*g2,xh2,r2)).astype(BF)
    yield
    S['a_proj'][...]+=dot_t(mixed,dst)
    yield
    dO=dot(wproj[...],dst).astype(BF)
    yield
    zr=jnp.zeros((16,TL),BF)
    dOtok=jnp.concatenate([dO[:,TL:],zr,dO[:,0:TL],zr],axis=0).T
    yield
    pr=mixf*dO.astype(F32)
    r16=lax.broadcasted_iota(jnp.int32,(16,TL),0)
    for w in range(2):
        for h in range(NH):
            k=3*w+h; ls=slice(k*TL,(k+1)*TL); ws=slice(TL*w,TL*w+TL); o=192*w
            d0,d1,d2=split3(-jnp.sum(pr[16*h:16*h+16,ws],axis=0,keepdims=True))
            W['oblk'][o+16*h:o+16*h+16,ls]=dO[16*h:16*h+16,ws]
            W['oblk'][o+48:o+64,ls]=jnp.where(r16==0,d0.astype(F32),jnp.where(r16==1,d1.astype(F32),jnp.where(r16==2,d2.astype(F32),0.0))).astype(BF)
            l0=64*(1-w)+16*h
            W['ot'][ls,:]=dOtok*lane_mask(l0)
            yield
    out(dst)

def backward(out, S, W, T):
    def bwd_dot(c):
        rs=slice(0,64) if c<4 else (slice(0,256) if c==4 else slice(128,256))
        return dot(W['tokv'][0:KP,rs],W['oblk'][rs,256*c:256*c+256]).astype(BF)
    dqp=[]
    dp=bwd_dot(0)
    for c in range(9):
        yield
        nxt=bwd_dot(c+1) if c<8 else None
        cs=slice(256*c,256*c+256)
        ds=W['P'][:,cs]*dp
        T['D'][:,cs]=ds
        yield
        dqp.append(dot(W['kT'][heads_of(c),0:KP],ds))
        dp=nxt
    dq=(0.25*spread(dqp)).astype(BF)
    yield
    def over_queries(a,b):
        t=None
        for i in range(3):
            ks=slice(768*i,768*i+768)
            d=dot(a[:,ks],b[ks,:])
            t=d if t is None else t+d
            yield t
    for t in over_queries(W['P'],W['ot']):
        yield
    T['dkv'][0:KP,128:256]=t.astype(BF)
    for t in over_queries(T['D'],W['qt']):
        yield
    T['dkv'][0:KP,0:128]=(0.25*t).astype(BF)
    yield
    dk=T['dkv'][:,0:128].T; dv=T['dkv'][:,128:256].T
    dpack=jnp.concatenate([dq,jnp.concatenate([dk[64:112],dk[0:48]],axis=1),jnp.concatenate([dv[64:112],dv[0:48]],axis=1)],axis=0)
    yield
    S['a_qkv'][...]+=dot_t(W['n1'][...],dpack)
    out(dpack)

def finish(x, dpack, dst, S, wqkv):
    g1=S['g1'][...]
    xh1,r1=norm(x)
    dn1=dot(wqkv[...],dpack).astype(BF).astype(F32)
    return (dst.astype(F32)+norm_back(dn1*g1,xh1,r1)).astype(BF)


def drive(timed):
    t=0
    live=list(timed)
    while live:
        left=[]
        for start,g in live:
            if t>=start:
                try:
                    next(g)
                except StopIteration:
                    continue
            left.append((start,g))
        live=left
        t+=1


G1 = 8
G2 = 16
ROWS = 32
TWO = sorted(
    ((a, b) for a in range(4) for b in range(4) if a or b), key=lambda s: -sum(min(v, 4 - v) for v in s)
)
NP = 3
S_KEYS = tuple(scratch())
W_KEYS = tuple(win_scratch())
T_KEYS = tuple(tmp_scratch())


def comm_scratch(nx, ny):
    return dict(
        grid=pltpu.VMEM((WIN, 24, LW), F32),
        rows=pltpu.VMEM((NWY, 64, LW), F32),
        xs=pltpu.VMEM((NWY, 32, LW), BF),
        xr=pltpu.VMEM((NWY, 32, LW), BF),
        ys=pltpu.VMEM((16, LW), BF),
        yr=pltpu.VMEM((16, LW), BF),
        ds=pltpu.VMEM((16, LW), BF),
        dr=pltpu.VMEM((16, LW), BF),
        xwin=pltpu.VMEM((NWY * NP, C, 2 * TL), BF),
        dpk=pltpu.VMEM((NWY * NP, 3 * C, 2 * TL), BF),
        dst=pltpu.VMEM((NWY * NP, C, 2 * TL), BF),
        sg=pltpu.VMEM((8, 2 * TL), F32),
        zt=pltpu.VMEM((LAB, 128), BF),
        back=pltpu.VMEM((NWY, 64, WIDTH), F32),
        bxs=pltpu.VMEM((NWY, 32, WIDTH), BF),
        bxr=pltpu.VMEM((NWY, 32, WIDTH), BF),
        bys=pltpu.VMEM((16, WIDTH), BF),
        byr=pltpu.VMEM((16, WIDTH), BF),
        bds=pltpu.VMEM((16, WIDTH), BF),
        bdr=pltpu.VMEM((16, WIDTH), BF),
        tmp=pltpu.VMEM((64, WIDTH), F32),
        outf=pltpu.VMEM((WIN, 24, WIDTH), F32),
        part=pltpu.VMEM((G1, ROWS, 128), F32),
        r1=pltpu.VMEM((G1 - 1, ROWS, 128), F32),
        r2=pltpu.VMEM((G2, ROWS, 128), BF),
        total=pltpu.VMEM((G1, ROWS, 128), F32),
        hs=pltpu.SemaphoreType.DMA((NWY + 2,)),
        hr=pltpu.SemaphoreType.DMA((NWY + 2,)),
        bs=pltpu.SemaphoreType.DMA((NWY + 2,)),
        br=pltpu.SemaphoreType.DMA((NWY + 2,)),
        s1=pltpu.SemaphoreType.DMA((G1 - 1,)),
        q1=pltpu.SemaphoreType.DMA((G1 - 1,)),
        s2=pltpu.SemaphoreType.DMA((G2 - 1,)),
        q2=pltpu.SemaphoreType.DMA((G2 - 1,)),
        s3=pltpu.SemaphoreType.DMA((G1 - 1,)),
        q3=pltpu.SemaphoreType.DMA((G1 - 1,)),
    )


def remote(src, dst, ssem, rsem, to):
    return pltpu.make_async_remote_copy(
        src_ref=src, dst_ref=dst, send_sem=ssem, recv_sem=rsem, device_id=to, device_id_type=MESH
    )


def make_kernel(nx, ny, tokens):
    c_keys = tuple(comm_scratch(nx, ny))

    def kernel(feat, lab, wqkv, wproj, wup, wdown, whead, g1, g2, *refs):
        out, o_sum = refs[:2]
        refs = refs[2:]
        S = dict(zip(S_KEYS, refs))
        refs = refs[len(S_KEYS):]
        Ws = [dict(zip(W_KEYS, refs[i * len(W_KEYS):])) for i in range(NP)]
        refs = refs[NP * len(W_KEYS):]
        Ts = [dict(zip(T_KEYS, refs[i * len(T_KEYS):])) for i in range(NP)]
        Q = dict(zip(c_keys, refs[NP * len(T_KEYS):]))
        mx = lax.axis_index("gx")
        my = lax.axis_index("gy")

        def at(dx, dy):
            return (lax.rem(mx + dx + nx, nx), lax.rem(my + dy + ny, ny))

        half = lax.rem(lax.div(mx, 2), 2)
        core = lax.rem(mx, 2)
        px = lax.div(mx, 4)
        m1 = px * 2 + core
        m2 = half * ny + my

        def in_one(k):
            x2 = lax.rem(px + k // 2, 4)
            c2 = lax.rem(core + k % 2, 2)
            return x2 * 2 + c2, ((x2 * 2 + half) * 2 + c2, my)

        z = half * 2 + lax.div(my, 4)
        y = lax.rem(my, 4)

        def in_two(k):
            dz, dy = TWO[k - 1]
            z2, y2 = lax.rem(z + dz, 4), lax.rem(y + dy, 4)
            return ((px * 2 + lax.div(z2, 2)) * 2 + core, lax.rem(z2, 2) * 4 + y2)

        barrier = pltpu.get_barrier_semaphore()
        peers = [at(1, 0), at(-1, 0), at(1, 1), at(-1, -1)]
        peers += [in_one(k)[1] for k in range(1, G1)] + [in_two(k) for k in range(1, G2)]
        for p in peers:
            pl.semaphore_signal(barrier, inc=1, device_id=p, device_id_type=MESH)

        grid = Q["grid"]
        tmp = Q["rows"]

        def widen(x0, x1):
            n = x1 - x0
            grid[x0:x1, 0:21, 0:WIDTH] = feat[x0:x1].astype(F32)
            grid[x0:x1, 0:21, WIDTH:LAB] = jnp.zeros((n, 21, LAB - WIDTH), F32)
            grid[x0:x1, 0:21, LAB:LW] = jnp.zeros((n, 21, LW - LAB), F32)
            grid[x0:x1, 0:21, LAB:LAB + DEPTH] = lab[x0:x1].astype(F32)

        def pack(wy):
            n = WIN if wy < 2 else 4
            for k in range(SHIFT):
                tmp[wy, 7 * k:7 * k + n, :] = grid[k, 7 * wy + 3:7 * wy + 3 + n, :]
            Q["xs"][wy] = tmp[wy, 0:32, :].astype(BF)

        hs, hr = Q["hs"], Q["hr"]
        xcopy = [remote(Q["xs"].at[w], Q["xr"].at[w], hs.at[w], hr.at[w], at(-1, 0)) for w in range(NWY)]
        ycopy = remote(Q["ys"], Q["yr"], hs.at[3], hr.at[3], at(0, -1))
        dcopy = remote(Q["ds"], Q["dr"], hs.at[4], hr.at[4], at(-1, -1))
        widen(0, SHIFT)
        pack(0)
        pl.semaphore_wait(barrier, len(peers))
        xcopy[0].start()
        widen(SHIFT, WIN)
        pack(1)
        pack(2)
        for k in range(4):
            tmp[0, 3 * k:3 * k + 3, :] = grid[3 + k, 0:3, :]
        Q["ys"][...] = tmp[0, 0:16, :].astype(BF)
        for k in range(SHIFT):
            tmp[1, 3 * k:3 * k + 3, :] = grid[k, 0:3, :]
        Q["ds"][...] = tmp[1, 0:16, :].astype(BF)

        init(S, Ws, Ts, wqkv, wproj, wup, wdown, whead, g1, g2)
        rows = Q["rows"]
        for wy in range(NWY):
            n = WIN if wy < 2 else 4
            for k in range(4):
                rows[wy, 7 * k:7 * k + n, :] = grid[3 + k, 7 * wy + 3:7 * wy + 3 + n, :]
            rows[wy, 48:64, :] = jnp.zeros((16, LW), F32)
        Q["zt"][...] = jnp.zeros((LAB, 128), BF)

        act_x = (mx == nx - 1).astype(F32)
        last_y = my == ny - 1
        lanes = lax.broadcasted_iota(jnp.int32, (1, TL), 1)

        xcopy[0].wait()
        xcopy[1].start()
        xcopy[2].start()
        ycopy.start()
        dcopy.start()

        def send_back(w):
            return remote(Q["bxs"].at[w], Q["bxr"].at[w], Q["bs"].at[w], Q["br"].at[w], at(1, 0))

        def tail(w):
            for p in range(NP):
                v = finish(Q["xwin"][NP * w + p].astype(F32), Q["dpk"][NP * w + p], Q["dst"][NP * w + p], S, wqkv)
                for i in range(2):
                    for j in range(WIN):
                        z = (7 * (2 * p + i) + j + SHIFT) % DEPTH
                        Q["zt"][C * z:C * z + C, 0:49] = v[:, TL * i + 49 * j:TL * i + 49 * j + 49]
                    yield
            flat = Q["zt"][...].T.astype(F32)[0:64, 0:WIDTH]
            Q["back"][w] = flat
            yield
            Q["bxs"][w] = jnp.concatenate([flat[28:49], jnp.zeros((11, WIDTH), F32)], axis=0).astype(BF)

        def step(wy, _):
            @pl.when(wy > 0)
            def _():
                remote(Q["xs"].at[wy], Q["xr"].at[wy], hs.at[wy], hr.at[wy], at(-1, 0)).wait()

            rows[wy, 28:49, :] = Q["xr"][wy].astype(F32)[0:21]

            @pl.when(wy == 2)
            def _():
                ycopy.wait()
                dcopy.wait()
                Q["tmp"][0:16, :] = Q["yr"][:, 0:WIDTH].astype(F32)
                Q["tmp"][16:32, :] = Q["dr"][:, 0:WIDTH].astype(F32)
                yl = Q["yr"][:, LAB:LW].astype(F32)
                dl = Q["dr"][:, LAB:LW].astype(F32)
                for k in range(4):
                    rows[2, 7 * k + 4:7 * k + 7, 0:WIDTH] = Q["tmp"][3 * k:3 * k + 3, :]
                    rows[2, 7 * k + 4:7 * k + 7, LAB:LW] = yl[3 * k:3 * k + 3]
                for k in range(SHIFT):
                    rows[2, 28 + 7 * k + 4:28 + 7 * k + 7, 0:WIDTH] = Q["tmp"][16 + 3 * k:16 + 3 * k + 3, :]
                    rows[2, 28 + 7 * k + 4:28 + 7 * k + 7, LAB:LW] = dl[3 * k:3 * k + 3]

            cols = rows[wy].astype(BF).T
            zero = jnp.zeros((C, TL - PT), BF)
            zrow = jnp.zeros((1, TL - PT), F32)
            for p in range(NP):
                zs = [[(7 * wz + j + SHIFT) % DEPTH for j in range(WIN)] for wz in (2 * p, 2 * p + 1)]
                halves = [jnp.concatenate([cols[C * z:C * z + C, 0:49] for z in w] + [zero], axis=1) for w in zs]
                Q["xwin"][NP * wy + p] = jnp.concatenate(halves, axis=1)
                marks = [
                    jnp.concatenate([cols[LAB + z:LAB + z + 1, 0:49].astype(F32) for z in w] + [zrow], axis=1)
                    for w in zs
                ]
                Q["sg"][p:p + 1, :] = jnp.concatenate(
                    [jnp.where(lanes < PT, 1.0 - 2.0 * m, 0.0) for m in marks], axis=1
                )

            gens, later = [], []
            act_y = jnp.logical_and(last_y, wy == 2).astype(F32)
            for p in range(NP):
                def put_dst(dst, p=p):
                    Q["dst"][NP * wy + p] = dst

                def put_dpk(dpack, p=p):
                    Q["dpk"][NP * wy + p] = dpack

                def get(p=p):
                    return Q["xwin"][NP * wy + p].astype(F32)

                act = (act_x, act_y, F32(0.0), F32(1.0 if p == NP - 1 else 0.0))
                gens.append((p, window(put_dst, get, Q["sg"][p:p + 1, :], act, S, Ws[p], Ts[p], wproj, wup)))
                later.append((p, backward(put_dpk, S, Ws[p], Ts[p])))
            before = lax.rem(wy + 2, 3)
            drive(gens + [(6, tail(before))])

            @pl.when(wy > 0)
            def _():
                send_back(before).start()

            drive(later)
            return 0

        lax.fori_loop(0, NWY, step, 0)

        a_head = jnp.sum(S["a_head"][...], axis=1, keepdims=True)
        acc = jnp.concatenate(
            [S["a_up"][...], S["a_down"][...], S["a_qkv"][...], S["a_proj"][...], a_head, jnp.zeros((C, 63), F32)],
            axis=1,
        )
        part = Q["part"]
        for j in range(16):
            if j < 15:
                v = acc[16 * (j % 3):16 * (j % 3) + 16, 128 * (j // 3):128 * (j // 3) + 128]
            else:
                v = jnp.zeros((16, 128), F32)
            part[j // 2, 16 * (j % 2):16 * (j % 2) + 16, :] = v
        first = []
        for k in range(1, G1):
            slot, to = in_one(k)
            first.append(remote(part.at[slot], Q["r1"].at[k - 1], Q["s1"].at[k - 1], Q["q1"].at[k - 1], to))
        for c in first:
            c.start()

        drive([(0, tail(2))])
        send_back(2).start()
        back, tmp = Q["back"], Q["tmp"]
        for k in range(4):
            tmp[3 * k:3 * k + 3, :] = back[2, 7 * k + 4:7 * k + 7, :]
        for k in range(SHIFT):
            tmp[16 + 3 * k:16 + 3 * k + 3, :] = back[2, 28 + 7 * k + 4:28 + 7 * k + 7, :]
        Q["bys"][...] = tmp[0:16, :].astype(BF)
        Q["bds"][...] = tmp[16:32, :].astype(BF)
        bycopy = remote(Q["bys"], Q["byr"], Q["bs"].at[3], Q["br"].at[3], at(0, 1))
        bdcopy = remote(Q["bds"], Q["bdr"], Q["bs"].at[4], Q["br"].at[4], at(1, 1))
        bycopy.start()
        bdcopy.start()

        for c in first:
            c.wait()
        csum = part[m1]
        for k in range(G1 - 1):
            csum = csum + Q["r1"][k]
        r2 = Q["r2"]
        r2[m2] = csum.astype(BF)
        second = [
            remote(r2.at[m2], r2.at[m2], Q["s2"].at[k - 1], Q["q2"].at[k - 1], in_two(k)) for k in range(1, G2)
        ]
        for c in second:
            c.start()

        outf = Q["outf"]
        for x in range(SHIFT, WIN):
            k = x - SHIFT
            for wy in range(NWY):
                n = WIN if wy < 2 else 4
                outf[x, 7 * wy + 3:7 * wy + 3 + n, :] = back[wy, 7 * k:7 * k + n, :]

        for c in second:
            c.wait()
        ctot = r2[0].astype(F32)
        for k in range(1, G2):
            ctot = ctot + r2[k].astype(F32)
        total = Q["total"]
        total[m1] = ctot * (1.0 / math.sqrt(tokens))
        third = [
            remote(total.at[m1], total.at[m1], Q["s3"].at[k - 1], Q["q3"].at[k - 1], in_one(k)[1])
            for k in range(1, G1)
        ]
        for c in third:
            c.start()

        bycopy.wait()
        bdcopy.wait()
        tmp[0:16, :] = Q["byr"][...].astype(F32)
        tmp[16:32, :] = Q["bdr"][...].astype(F32)
        for k in range(4):
            outf[SHIFT + k, 0:3, :] = tmp[3 * k:3 * k + 3, :]
        for k in range(SHIFT):
            outf[k, 0:3, :] = tmp[16 + 3 * k:16 + 3 * k + 3, :]
        for wy in range(NWY):
            send_back(wy).wait()
            n = WIN if wy < 2 else 4
            tmp[32:64, :] = Q["bxr"][wy].astype(F32)
            for k in range(SHIFT):
                outf[k, 7 * wy + 3:7 * wy + 3 + n, :] = tmp[32 + 7 * k:32 + 7 * k + n, :]
        out[...] = outf[:, 0:21, :].astype(BF)

        for c in third:
            c.wait()
        parts = []
        for l in range(5):
            parts.append(
                jnp.concatenate(
                    [total[j // 2, 16 * (j % 2):16 * (j % 2) + 16, :] for j in range(3 * l, 3 * l + 3)], axis=0
                )
            )
        whole = jnp.concatenate(parts, axis=1)
        o_sum[...] = whole

    return kernel


def deliver(back, sums, out, o_qkv, o_proj, o_up, o_down, o_head):
    out[...] = back[...]
    o_up[...] = sums[:, 0:192]
    o_down[...] = sums[:, 192:384]
    o_qkv[...] = sums[:, 384:528]
    o_proj[...] = sums[:, 528:576]
    col = sums[:, 512:640].T[64:65]
    o_head[...] = jnp.concatenate([-col, col], axis=0)


def body(features, labels, gain_one, gain_two, w_qkv, w_proj, w_up, w_down, w_head):
    nx, ny = lax.axis_size("gx"), lax.axis_size("gy")
    tokens = nx * ny * features.shape[0] * features.shape[1] * DEPTH
    vmem = pl.BlockSpec(memory_space=pltpu.VMEM)
    back, sums = pl.pallas_call(
        make_kernel(nx, ny, tokens),
        out_shape=[jax.ShapeDtypeStruct(features.shape, BF), jax.ShapeDtypeStruct((C, 640), F32)],
        in_specs=[vmem] * 9,
        out_specs=[vmem] * 2,
        scratch_shapes=list(scratch().values())
        + list(win_scratch().values()) * NP
        + list(tmp_scratch().values()) * NP
        + list(comm_scratch(nx, ny).values()),
        compiler_params=pltpu.CompilerParams(
            collective_id=0, has_side_effects=True, vmem_limit_bytes=60 * 2**20
        ),
    )(
        features, labels, w_qkv, w_proj, w_up, w_down.T, w_head.T,
        gain_one.reshape(1, C), gain_two.reshape(1, C),
    )
    out, d_qkv, d_proj, d_up, d_down, d_head = pl.pallas_call(
        deliver,
        out_shape=[jax.ShapeDtypeStruct(features.shape, BF)] + [
            jax.ShapeDtypeStruct(s, F32) for s in ((C, 144), (C, C), (C, FF), (C, FF), (2, C))
        ],
        in_specs=[vmem] * 2,
        out_specs=[vmem] * 6,
    )(back, sums)
    return out, d_qkv, d_proj, d_up, d_down.T, d_head.T


def solution(mesh):
    placed = (P("gx", "gy", None), P("gx", "gy", None), P(), P(), P(), P(), P(), P(), P())
    return jax.shard_map(
        body,
        mesh=mesh,
        in_specs=placed,
        out_specs=(P("gx", "gy", None), P(), P(), P(), P(), P()),
        check_vma=False,
    )
```

```python
import math

import jax
import jax.numpy as jnp
from jax import lax
from jax.experimental import pallas as pl
from jax.experimental.pallas import tpu as pltpu
from jax.sharding import PartitionSpec as P

BF = jnp.bfloat16
F32 = jnp.float32
C = 48
FF = 192
NH = 3
WIN = 7
SHIFT = 3
DEPTH = 42
WIDTH = DEPTH * C
LAB = 2048
LW = 2176
KP = 352
TL = 384
PT = 343
NZ = 6
NWY = 3
EPS = 1e-5
BIG = 2.0**100
LOG2E_4 = 0.25 * math.log2(math.e)
CH = [(0, 256), (256, 512), (512, 768), (768, 1024), (1024, 1152)]
GC1 = math.sqrt(2 / math.pi)
GC2 = 0.044715 * GC1
MESH = pl.DeviceIdType.MESH


def dot(a,b): return lax.dot_general(a,b,(((1,),(0,)),((),())),preferred_element_type=F32)
def dot_t(a,b): return lax.dot_general(a,b,(((1,),(1,)),((),())),preferred_element_type=F32)
def split3(v):
    a=v.astype(BF); r=v-a.astype(F32); b=r.astype(BF); r=r-b.astype(F32); return a,b,r.astype(BF)
def mean0(v): return jnp.sum(v,axis=0,keepdims=True)*(1.0/C)
def norm(v):
    s=v-mean0(v)
    r=lax.rsqrt(mean0(s*s)+EPS)
    return s*r, r
def norm_back(d,xh,r):
    return (d-mean0(d)-xh*mean0(d*xh))*r

def scratch():
    return dict(
      qkvT=pltpu.VMEM((144,C),BF), projT=pltpu.VMEM((C,C),BF), upT=pltpu.VMEM((FF,C),BF), downT=pltpu.VMEM((C,FF),BF), down=pltpu.VMEM((FF,C),BF),
      wx=pltpu.VMEM((128,512),BF), kmask=pltpu.VMEM((16,TL),BF), qmask=pltpu.VMEM((16,TL),F32),
      g1=pltpu.VMEM((C,1),F32), g2=pltpu.VMEM((C,1),F32), wd=pltpu.VMEM((C,1),F32),
      a_up=pltpu.VMEM((C,FF),F32), a_down=pltpu.VMEM((C,FF),F32), a_qkv=pltpu.VMEM((C,144),F32), a_proj=pltpu.VMEM((C,C),F32), a_head=pltpu.VMEM((C,128),F32),
    )
def win_scratch():
    return dict(oblk=pltpu.VMEM((256,2304),BF), P=pltpu.VMEM((KP,2304),BF),
       qt=pltpu.VMEM((2304,128),BF), ot=pltpu.VMEM((2304,128),BF), tokv=pltpu.VMEM((TL,256),BF), kT=pltpu.VMEM((96,TL),BF), n1=pltpu.VMEM((C,2*TL),BF))

def tmp_scratch():
    return dict(qblk=pltpu.VMEM((240,2304),BF), D=pltpu.VMEM((KP,2304),BF), dkv=pltpu.VMEM((TL,256),BF))

def init(S, Ws, Ts, wqkv, wproj, wup, wdownT, whT, g1, g2):
    S['qkvT'][...]=wqkv[...].T
    S['projT'][...]=wproj[...].T
    S['upT'][...]=wup[...].T
    S['downT'][...]=wdownT[...]
    S['down'][...]=wdownT[...].T
    wq=wqkv[...].astype(F32)
    wk=wq[:,48:96]; wv=wq[:,96:144]
    z=lambda n: jnp.zeros((C,n),F32)
    r=lax.broadcasted_iota(jnp.int32,(16,512),0); l=lax.broadcasted_iota(jnp.int32,(16,512),1)
    wqq=wq[:,0:48]
    rows_a=jnp.concatenate([wk,wk,z(160),wv,z(16),wqq,z(144)],axis=1)
    mask_a=((l==96+r)|((l>=304)&(l<307)&(r==7))).astype(F32)
    rows_b=jnp.concatenate([z(128),wk,wk,z(160),wqq,z(16),wv,z(16)],axis=1)
    mask_b=((l==224+r)|((l>=496)&(l<499)&(r==7))).astype(F32)
    S['wx'][...]=jnp.concatenate([rows_a,mask_a,rows_b,mask_b],axis=0).astype(BF)
    t=lax.broadcasted_iota(jnp.int32,(16,TL),1); r=lax.broadcasted_iota(jnp.int32,(16,TL),0)
    bz=(t>=4*49).astype(F32)
    u=t-49*sum((t>=49*k).astype(jnp.int32) for k in range(1,7))
    bx=(u>=28).astype(F32)
    v=u-7*sum((u>=7*k).astype(jnp.int32) for k in range(1,7))
    by=(v>=4).astype(F32)
    b=jnp.where(r<2,bx,jnp.where(r<4,by,bz))
    first=(r%2)==0
    S['kmask'][...]=jnp.where(r<6,jnp.where(first,1.0-b,b),jnp.where(r==6,(t>=343).astype(F32),(r==7).astype(F32))).astype(BF)
    S['qmask'][...]=jnp.where(r<6,jnp.where(first,b,1.0-b),(r==6).astype(F32))*(-BIG)
    wh=whT[...].astype(F32)
    cols=jnp.concatenate([g1[...],g2[...],wh[1:2]-wh[0:1],jnp.zeros((5,C),F32)],axis=0)
    cols=jnp.concatenate([cols,jnp.zeros((8,128-C),F32)],axis=1).T
    S['g1'][...]=cols[0:C,0:1]; S['g2'][...]=cols[0:C,1:2]; S['wd'][...]=cols[0:C,2:3]
    for k in ('a_up','a_down','a_qkv','a_proj','a_head'): S[k][...]=jnp.zeros(S[k].shape,F32)
    for w in Ws:
        w['oblk'][...]=jnp.zeros((256,2304),BF)
    for t in Ts:
        t['qblk'][...]=jnp.zeros((240,2304),BF)
        t['dkv'][...]=jnp.zeros((TL,256),BF)

def lane_mask(l0):
    lane=lax.broadcasted_iota(jnp.int32,(1,128),1)
    return jnp.where((lane>=l0)&(lane<l0+16),1.0,0.0).astype(BF)

def split2(v):
    a=v.astype(BF); return a,(v-a.astype(F32)).astype(BF)

def spread(parts):
    def block(j):
        c=j//2; k0=256*c//TL; k=j//3
        return parts[c][16*(k-k0):16*(k-k0)+16,128*(j%2):128*(j%2)+128]
    cols=[jnp.concatenate([block(3*k+i) for i in range(3)],axis=1) for k in range(6)]
    return jnp.concatenate([jnp.concatenate(cols[0:3],axis=0),jnp.concatenate(cols[3:6],axis=0)],axis=1)

def heads_of(c):
    return slice(16*(256*c//TL),16*((256*c+255)//TL)+16)

def window(out, x, sign, act, S, W, T, wproj, wup):
    x=x()
    g1=S['g1'][...]; g2=S['g2'][...]; wd=S['wd'][...]
    n1=(norm(x)[0]*g1).astype(BF)
    yield
    packT=dot(S['qkvT'][...],n1).astype(BF)
    yield
    km=S['kmask'][...]
    tok=dot(jnp.concatenate([n1[:,0:TL],km,n1[:,TL:],km],axis=0).T, S['wx'][...]).astype(BF)
    yield
    qs=split2(packT[0:48].astype(F32)*LOG2E_4)
    r=lax.broadcasted_iota(jnp.int32,(16,1),0)
    W['n1'][...]=n1
    W['tokv'][...]=tok[:,256:512]
    for w in range(2):
        W['kT'][48*w:48*w+48,:]=packT[48:96,TL*w:TL*w+TL]
    yield
    for w in range(2):
        sc=jnp.where(r<2,act[0],jnp.where(r<4,act[1],jnp.where(r<6,act[2+w],1.0)))
        qm=(S['qmask'][...]*sc).astype(BF)
        qtok=tok[:,256+128*w:384+128*w]
        for h in range(NH):
            k=3*w+h; ls=slice(k*TL,(k+1)*TL)
            for i in range(2):
                T['qblk'][128*w+48*i+16*h:128*w+48*i+16*h+16,ls]=qs[i][16*h:16*h+16,TL*w:TL*w+TL]
            T['qblk'][128*w+96:128*w+112,ls]=qm
            l0=64*(1-w)+16*h
            W['qt'][ls,:]=qtok*lane_mask(l0)
            yield
    tk=tok[:KP]
    vT=jnp.concatenate([packT[96:144,0:KP],packT[96:144,TL:TL+KP]],axis=0)
    def fwd_dot(c):
        rs=slice(0,112) if c<4 else (slice(0,240) if c==4 else slice(128,240))
        return jnp.exp2(dot(tk[:,rs],T['qblk'][rs,256*c:256*c+256]))
    mixp=[]
    p=fwd_dot(0)
    for c in range(9):
        yield
        nxt=fwd_dot(c+1) if c<8 else None
        P=(p*(1.0/jnp.sum(p,axis=0,keepdims=True))).astype(BF)
        W['P'][:,256*c:256*c+256]=P
        yield
        mixp.append(dot(vT[heads_of(c)],P))
        p=nxt
    mixf=spread(mixp)
    mixed=mixf.astype(BF)
    ao=dot(S['projT'][...],mixed).astype(BF).astype(F32)
    yield
    state=(x+ao).astype(BF).astype(F32)
    xh2,r2=norm(state)
    n2=(xh2*g2).astype(BF)
    yield
    hh=dot(S['upT'][...],n2)
    yield
    h2=hh*hh
    t=jnp.tanh(hh*(GC1+GC2*h2))
    s=0.5+0.5*t
    inf=hh*s
    inner=inf.astype(BF)
    dg=s+inf*(1.0-s)*(2*GC1+6*GC2*h2)
    yield
    res=(state+dot(S['downT'][...],inner)).astype(BF).astype(F32)
    yield
    z=jnp.sum(res*wd,axis=0,keepdims=True)
    g=sign*(1.0/(1.0+jnp.exp(-z*sign)))
    rg=res*g
    S['a_head'][...]+=sum(rg[:,128*i:128*i+128] for i in range(1,6))+rg[:,0:128]
    dres=(wd*g).astype(BF)
    yield
    dinner=dot(S['down'][...],dres).astype(BF).astype(F32)
    yield
    S['a_down'][...]+=dot_t(dres,inner)
    yield
    dh=(dinner*dg).astype(BF)
    yield
    S['a_up'][...]+=dot_t(n2,dh)
    yield
    dn2=dot(wup[...],dh).astype(BF).astype(F32)
    yield
    dst=(dres.astype(F32)+norm_back(dn2*g2,xh2,r2)).astype(BF)
    yield
    S['a_proj'][...]+=dot_t(mixed,dst)
    yield
    dO=dot(wproj[...],dst).astype(BF)
    yield
    zr=jnp.zeros((16,TL),BF)
    dOtok=jnp.concatenate([dO[:,TL:],zr,dO[:,0:TL],zr],axis=0).T
    yield
    pr=mixf*dO.astype(F32)
    r16=lax.broadcasted_iota(jnp.int32,(16,TL),0)
    for w in range(2):
        for h in range(NH):
            k=3*w+h; ls=slice(k*TL,(k+1)*TL); ws=slice(TL*w,TL*w+TL); o=192*w
            d0,d1,d2=split3(-jnp.sum(pr[16*h:16*h+16,ws],axis=0,keepdims=True))
            W['oblk'][o+16*h:o+16*h+16,ls]=dO[16*h:16*h+16,ws]
            W['oblk'][o+48:o+64,ls]=jnp.where(r16==0,d0.astype(F32),jnp.where(r16==1,d1.astype(F32),jnp.where(r16==2,d2.astype(F32),0.0))).astype(BF)
            l0=64*(1-w)+16*h
            W['ot'][ls,:]=dOtok*lane_mask(l0)
            yield
    out(dst)

def backward(out, S, W, T):
    def bwd_dot(c):
        rs=slice(0,64) if c<4 else (slice(0,256) if c==4 else slice(128,256))
        return dot(W['tokv'][0:KP,rs],W['oblk'][rs,256*c:256*c+256]).astype(BF)
    dqp=[]
    dp=bwd_dot(0)
    for c in range(9):
        yield
        nxt=bwd_dot(c+1) if c<8 else None
        cs=slice(256*c,256*c+256)
        ds=W['P'][:,cs]*dp
        T['D'][:,cs]=ds
        yield
        dqp.append(dot(W['kT'][heads_of(c),0:KP],ds))
        dp=nxt
    dq=(0.25*spread(dqp)).astype(BF)
    yield
    def over_queries(a,b):
        t=None
        for i in range(3):
            ks=slice(768*i,768*i+768)
            d=dot(a[:,ks],b[ks,:])
            t=d if t is None else t+d
            yield t
    for t in over_queries(W['P'],W['ot']):
        yield
    T['dkv'][0:KP,128:256]=t.astype(BF)
    for t in over_queries(T['D'],W['qt']):
        yield
    T['dkv'][0:KP,0:128]=(0.25*t).astype(BF)
    yield
    dk=T['dkv'][:,0:128].T; dv=T['dkv'][:,128:256].T
    dpack=jnp.concatenate([dq,jnp.concatenate([dk[64:112],dk[0:48]],axis=1),jnp.concatenate([dv[64:112],dv[0:48]],axis=1)],axis=0)
    yield
    S['a_qkv'][...]+=dot_t(W['n1'][...],dpack)
    out(dpack)

def finish(x, dpack, dst, S, wqkv):
    g1=S['g1'][...]
    xh1,r1=norm(x)
    dn1=dot(wqkv[...],dpack).astype(BF).astype(F32)
    return (dst.astype(F32)+norm_back(dn1*g1,xh1,r1)).astype(BF)


def drive(timed):
    t=0
    live=list(timed)
    while live:
        left=[]
        for start,g in live:
            if t>=start:
                try:
                    next(g)
                except StopIteration:
                    continue
            left.append((start,g))
        live=left
        t+=1


G1 = 8
G2 = 16
ROWS = 32
TWO = sorted(
    ((a, b) for a in range(4) for b in range(4) if a or b), key=lambda s: -sum(min(v, 4 - v) for v in s)
)
NP = 3
S_KEYS = tuple(scratch())
W_KEYS = tuple(win_scratch())
T_KEYS = tuple(tmp_scratch())


def comm_scratch(nx, ny):
    return dict(
        grid=pltpu.VMEM((WIN, 24, LW), F32),
        rows=pltpu.VMEM((NWY, 64, LW), F32),
        xs=pltpu.VMEM((NWY, 32, LW), BF),
        xr=pltpu.VMEM((NWY, 32, LW), BF),
        ys=pltpu.VMEM((16, LW), BF),
        yr=pltpu.VMEM((16, LW), BF),
        ds=pltpu.VMEM((16, LW), BF),
        dr=pltpu.VMEM((16, LW), BF),
        xwin=pltpu.VMEM((NWY * NP, C, 2 * TL), BF),
        dpk=pltpu.VMEM((NWY * NP, 3 * C, 2 * TL), BF),
        dst=pltpu.VMEM((NWY * NP, C, 2 * TL), BF),
        sg=pltpu.VMEM((8, 2 * TL), F32),
        zt=pltpu.VMEM((LAB, 128), BF),
        back=pltpu.VMEM((NWY, 64, WIDTH), F32),
        bxs=pltpu.VMEM((NWY, 32, WIDTH), BF),
        bxr=pltpu.VMEM((NWY, 32, WIDTH), BF),
        bzs=pltpu.VMEM((16, WIDTH), BF),
        bzr=pltpu.VMEM((16, WIDTH), BF),
        bys=pltpu.VMEM((16, WIDTH), BF),
        byr=pltpu.VMEM((16, WIDTH), BF),
        bds=pltpu.VMEM((16, WIDTH), BF),
        bdr=pltpu.VMEM((16, WIDTH), BF),
        tmp=pltpu.VMEM((64, WIDTH), F32),
        outf=pltpu.VMEM((WIN, 24, WIDTH), F32),
        part=pltpu.VMEM((G1, ROWS, 128), F32),
        r1=pltpu.VMEM((G1 - 1, ROWS, 128), F32),
        r2=pltpu.VMEM((G2, ROWS, 128), BF),
        total=pltpu.VMEM((G1, ROWS, 128), F32),
        w1=pltpu.VMEM((G1, 64, 128), BF),
        w2=pltpu.VMEM((G2, 64, 128), BF),
        hs=pltpu.SemaphoreType.DMA((NWY + 2,)),
        hr=pltpu.SemaphoreType.DMA((NWY + 2,)),
        bs=pltpu.SemaphoreType.DMA((NWY + 2,)),
        br=pltpu.SemaphoreType.DMA((NWY + 2,)),
        s1=pltpu.SemaphoreType.DMA((G1 - 1,)),
        q1=pltpu.SemaphoreType.DMA((G1 - 1,)),
        s2=pltpu.SemaphoreType.DMA((G2 - 1,)),
        q2=pltpu.SemaphoreType.DMA((G2 - 1,)),
        s3=pltpu.SemaphoreType.DMA((G1 - 1,)),
        q3=pltpu.SemaphoreType.DMA((G1 - 1,)),
        u1=pltpu.SemaphoreType.DMA((G1 - 1,)),
        v1=pltpu.SemaphoreType.DMA((G1 - 1,)),
        u2=pltpu.SemaphoreType.DMA((G2 - 1,)),
        v2=pltpu.SemaphoreType.DMA((G2 - 1,)),
    )


def remote(src, dst, ssem, rsem, to):
    return pltpu.make_async_remote_copy(
        src_ref=src, dst_ref=dst, send_sem=ssem, recv_sem=rsem, device_id=to, device_id_type=MESH
    )


def make_kernel(nx, ny, tokens):
    c_keys = tuple(comm_scratch(nx, ny))

    def kernel(feat, lab, wqkv, wproj, wup, wdown, whead, g1, g2, *refs):
        out, o_sum = refs[:2]
        refs = refs[2:]
        S = dict(zip(S_KEYS, refs))
        refs = refs[len(S_KEYS):]
        Ws = [dict(zip(W_KEYS, refs[i * len(W_KEYS):])) for i in range(NP)]
        refs = refs[NP * len(W_KEYS):]
        Ts = [dict(zip(T_KEYS, refs[i * len(T_KEYS):])) for i in range(NP)]
        Q = dict(zip(c_keys, refs[NP * len(T_KEYS):]))
        mx = lax.axis_index("gx")
        my = lax.axis_index("gy")

        def at(dx, dy):
            return (lax.rem(mx + dx + nx, nx), lax.rem(my + dy + ny, ny))

        half = lax.rem(lax.div(mx, 2), 2)
        core = lax.rem(mx, 2)
        px = lax.div(mx, 4)
        m1 = px * 2 + core
        m2 = half * ny + my

        def in_one(k):
            x2 = lax.rem(px + k // 2, 4)
            c2 = lax.rem(core + k % 2, 2)
            return x2 * 2 + c2, ((x2 * 2 + half) * 2 + c2, my)

        z = half * 2 + lax.div(my, 4)
        y = lax.rem(my, 4)

        def in_two(k):
            dz, dy = TWO[k - 1]
            z2, y2 = lax.rem(z + dz, 4), lax.rem(y + dy, 4)
            return ((px * 2 + lax.div(z2, 2)) * 2 + core, lax.rem(z2, 2) * 4 + y2)

        barrier = pltpu.get_barrier_semaphore()
        peers = [at(1, 0), at(-1, 0), at(1, 1), at(-1, -1)]
        peers += [in_one(k)[1] for k in range(1, G1)] + [in_two(k) for k in range(1, G2)]
        for p in peers:
            pl.semaphore_signal(barrier, inc=1, device_id=p, device_id_type=MESH)

        grid = Q["grid"]
        tmp = Q["rows"]

        def widen(x0, x1):
            n = x1 - x0
            grid[x0:x1, 0:21, 0:WIDTH] = feat[x0:x1].astype(F32)
            grid[x0:x1, 0:21, WIDTH:LAB] = jnp.zeros((n, 21, LAB - WIDTH), F32)
            grid[x0:x1, 0:21, LAB:LW] = jnp.zeros((n, 21, LW - LAB), F32)
            grid[x0:x1, 0:21, LAB:LAB + DEPTH] = lab[x0:x1].astype(F32)

        def pack(wy):
            n = WIN if wy < 2 else 4
            for k in range(SHIFT):
                tmp[wy, 7 * k:7 * k + n, :] = grid[k, 7 * wy + 3:7 * wy + 3 + n, :]
            Q["xs"][wy] = tmp[wy, 0:32, :].astype(BF)

        hs, hr = Q["hs"], Q["hr"]
        xcopy = [remote(Q["xs"].at[w], Q["xr"].at[w], hs.at[w], hr.at[w], at(-1, 0)) for w in range(NWY)]
        ycopy = remote(Q["ys"], Q["yr"], hs.at[3], hr.at[3], at(0, -1))
        dcopy = remote(Q["ds"], Q["dr"], hs.at[4], hr.at[4], at(-1, -1))
        widen(0, SHIFT)
        pack(0)
        pl.semaphore_wait(barrier, len(peers))
        xcopy[0].start()
        widen(SHIFT, WIN)
        pack(1)
        pack(2)
        for k in range(4):
            tmp[0, 3 * k:3 * k + 3, :] = grid[3 + k, 0:3, :]
        Q["ys"][...] = tmp[0, 0:16, :].astype(BF)
        for k in range(SHIFT):
            tmp[1, 3 * k:3 * k + 3, :] = grid[k, 0:3, :]
        Q["ds"][...] = tmp[1, 0:16, :].astype(BF)

        init(S, Ws, Ts, wqkv, wproj, wup, wdown, whead, g1, g2)
        rows = Q["rows"]
        for wy in range(NWY):
            n = WIN if wy < 2 else 4
            for k in range(4):
                rows[wy, 7 * k:7 * k + n, :] = grid[3 + k, 7 * wy + 3:7 * wy + 3 + n, :]
            rows[wy, 48:64, :] = jnp.zeros((16, LW), F32)
        Q["zt"][...] = jnp.zeros((LAB, 128), BF)

        act_x = (mx == nx - 1).astype(F32)
        last_y = my == ny - 1
        lanes = lax.broadcasted_iota(jnp.int32, (1, TL), 1)

        xcopy[0].wait()
        xcopy[1].start()
        xcopy[2].start()
        ycopy.start()
        dcopy.start()

        def send_back(w):
            return remote(Q["bxs"].at[w], Q["bxr"].at[w], Q["bs"].at[w], Q["br"].at[w], at(1, 0))

        def tail(w):
            for p in range(NP):
                v = finish(Q["xwin"][NP * w + p].astype(F32), Q["dpk"][NP * w + p], Q["dst"][NP * w + p], S, wqkv)
                for i in range(2):
                    for j in range(WIN):
                        z = (7 * (2 * p + i) + j + SHIFT) % DEPTH
                        Q["zt"][C * z:C * z + C, 0:49] = v[:, TL * i + 49 * j:TL * i + 49 * j + 49]
                    yield
            flat = Q["zt"][...].T.astype(F32)[0:64, 0:WIDTH]
            Q["back"][w] = flat
            yield
            Q["bxs"][w] = jnp.concatenate([flat[28:49], jnp.zeros((11, WIDTH), F32)], axis=0).astype(BF)

        def windows_of(w):
            cols = rows[w].astype(BF).T
            zero = jnp.zeros((C, TL - PT), BF)
            zrow = jnp.zeros((1, TL - PT), F32)
            for p in range(NP):
                zs = [[(7 * wz + j + SHIFT) % DEPTH for j in range(WIN)] for wz in (2 * p, 2 * p + 1)]
                halves = [jnp.concatenate([cols[C * z:C * z + C, 0:49] for z in u] + [zero], axis=1) for u in zs]
                Q["xwin"][NP * w + p] = jnp.concatenate(halves, axis=1)
                marks = [
                    jnp.concatenate([cols[LAB + z:LAB + z + 1, 0:49].astype(F32) for z in u] + [zrow], axis=1)
                    for u in zs
                ]
                Q["sg"][p:p + 1, :] = jnp.concatenate(
                    [jnp.where(lanes < PT, 1.0 - 2.0 * m, 0.0) for m in marks], axis=1
                )
                yield

        rows[0, 28:49, :] = Q["xr"][0].astype(F32)[0:21]
        drive([(0, windows_of(0))])

        part = Q["part"]

        def scatter():
            copies = []
            for k in range(1, G1):
                slot, to = in_one(k)
                copies.append(remote(part.at[slot], Q["r1"].at[k - 1], Q["s1"].at[k - 1], Q["q1"].at[k - 1], to))
            return copies

        def first_sums():
            a_head = jnp.sum(S["a_head"][...], axis=1, keepdims=True)
            acc = jnp.concatenate(
                [S["a_up"][...], S["a_down"][...], S["a_proj"][...], a_head, jnp.zeros((C, 79), F32)], axis=1
            )
            for j in range(16):
                if j < 12:
                    v = acc[16 * (j % 3):16 * (j % 3) + 16, 128 * (j // 3):128 * (j // 3) + 128]
                else:
                    v = jnp.zeros((16, 128), F32)
                part[j // 2, 16 * (j % 2):16 * (j % 2) + 16, :] = v

        def step(wy, _):
            gens, later = [], []
            act_y = jnp.logical_and(last_y, wy == 2).astype(F32)
            for p in range(NP):
                def put_dst(dst, p=p):
                    Q["dst"][NP * wy + p] = dst

                def put_dpk(dpack, p=p):
                    Q["dpk"][NP * wy + p] = dpack

                def get(p=p):
                    return Q["xwin"][NP * wy + p].astype(F32)

                act = (act_x, act_y, F32(0.0), F32(1.0 if p == NP - 1 else 0.0))
                gens.append((p, window(put_dst, get, Q["sg"][p:p + 1, :], act, S, Ws[p], Ts[p], wproj, wup)))
                later.append((p, backward(put_dpk, S, Ws[p], Ts[p])))
            before = lax.rem(wy + 2, 3)
            drive(gens + [(6, tail(before))])

            @pl.when(wy > 0)
            def _():
                send_back(before).start()

            @pl.when(wy == 2)
            def _():
                first_sums()
                for c in scatter():
                    c.start()

            following = lax.rem(wy + 1, 3)

            @pl.when(wy < 2)
            def _():
                remote(
                    Q["xs"].at[following], Q["xr"].at[following], hs.at[following], hr.at[following], at(-1, 0)
                ).wait()
                rows[following, 28:49, :] = Q["xr"][following].astype(F32)[0:21]

            @pl.when(wy == 1)
            def _():
                ycopy.wait()
                dcopy.wait()
                Q["tmp"][0:16, :] = Q["yr"][:, 0:WIDTH].astype(F32)
                Q["tmp"][16:32, :] = Q["dr"][:, 0:WIDTH].astype(F32)
                yl = Q["yr"][:, LAB:LW].astype(F32)
                dl = Q["dr"][:, LAB:LW].astype(F32)
                for k in range(4):
                    rows[2, 7 * k + 4:7 * k + 7, 0:WIDTH] = Q["tmp"][3 * k:3 * k + 3, :]
                    rows[2, 7 * k + 4:7 * k + 7, LAB:LW] = yl[3 * k:3 * k + 3]
                for k in range(SHIFT):
                    rows[2, 28 + 7 * k + 4:28 + 7 * k + 7, 0:WIDTH] = Q["tmp"][16 + 3 * k:16 + 3 * k + 3, :]
                    rows[2, 28 + 7 * k + 4:28 + 7 * k + 7, LAB:LW] = dl[3 * k:3 * k + 3]

            drive(later + [(4, windows_of(following))])
            return 0

        lax.fori_loop(0, NWY, step, 0)

        w1, w2 = Q["w1"], Q["w2"]
        mine = S["a_qkv"][...].astype(BF)
        edge = jnp.concatenate(
            [mine[16 * g:16 * g + 16, 128:144] for g in range(3)] + [jnp.zeros((16, 80), BF)], axis=1
        )
        w1[m1] = jnp.concatenate([mine[:, 0:128], edge], axis=0)
        fourth = [
            remote(w1.at[m1], w1.at[m1], Q["u1"].at[k - 1], Q["v1"].at[k - 1], in_one(k)[1]) for k in range(1, G1)
        ]
        for c in fourth:
            c.start()

        for c in scatter():
            c.wait()
        csum = part[m1]
        for k in range(G1 - 1):
            csum = csum + Q["r1"][k]
        r2 = Q["r2"]
        r2[m2] = csum.astype(BF)
        second = [
            remote(r2.at[m2], r2.at[m2], Q["s2"].at[k - 1], Q["q2"].at[k - 1], in_two(k)) for k in range(1, G2)
        ]
        for c in second:
            c.start()

        drive([(0, tail(2))])
        back, tmp = Q["back"], Q["tmp"]
        for k in range(4):
            tmp[3 * k:3 * k + 3, :] = back[2, 7 * k + 4:7 * k + 7, :]
        for k in range(SHIFT):
            tmp[16 + 3 * k:16 + 3 * k + 3, :] = back[2, 28 + 7 * k + 4:28 + 7 * k + 7, :]
        for k in range(SHIFT):
            tmp[32 + 4 * k:36 + 4 * k, :] = back[2, 28 + 7 * k:28 + 7 * k + 4, :]
        Q["bzs"][...] = tmp[32:48, :].astype(BF)
        bzcopy = remote(Q["bzs"], Q["bzr"], Q["bs"].at[2], Q["br"].at[2], at(1, 0))
        Q["bys"][...] = tmp[0:16, :].astype(BF)
        Q["bds"][...] = tmp[16:32, :].astype(BF)
        bycopy = remote(Q["bys"], Q["byr"], Q["bs"].at[3], Q["br"].at[3], at(0, 1))
        bdcopy = remote(Q["bds"], Q["bdr"], Q["bs"].at[4], Q["br"].at[4], at(1, 1))
        bzcopy.start()
        bycopy.start()
        bdcopy.start()

        for c in fourth:
            c.wait()
        s8 = w1[0].astype(F32)
        for k in range(1, G1):
            s8 = s8 + w1[k].astype(F32)
        w2[m2] = s8.astype(BF)
        fifth = [
            remote(w2.at[m2], w2.at[m2], Q["u2"].at[k - 1], Q["v2"].at[k - 1], in_two(k)) for k in range(1, G2)
        ]
        for c in fifth:
            c.start()

        outf = Q["outf"]
        for x in range(SHIFT, WIN):
            k = x - SHIFT
            for wy in range(NWY):
                n = WIN if wy < 2 else 4
                outf[x, 7 * wy + 3:7 * wy + 3 + n, :] = back[wy, 7 * k:7 * k + n, :]

        for c in second:
            c.wait()
        ctot = r2[0].astype(F32)
        for k in range(1, G2):
            ctot = ctot + r2[k].astype(F32)
        total = Q["total"]
        total[m1] = ctot * (1.0 / math.sqrt(tokens))
        third = [
            remote(total.at[m1], total.at[m1], Q["s3"].at[k - 1], Q["q3"].at[k - 1], in_one(k)[1])
            for k in range(1, G1)
        ]
        for c in third:
            c.start()

        bycopy.wait()
        bdcopy.wait()
        tmp[0:16, :] = Q["byr"][...].astype(F32)
        tmp[16:32, :] = Q["bdr"][...].astype(F32)
        for k in range(4):
            outf[SHIFT + k, 0:3, :] = tmp[3 * k:3 * k + 3, :]
        for k in range(SHIFT):
            outf[k, 0:3, :] = tmp[16 + 3 * k:16 + 3 * k + 3, :]
        for wy in range(2):
            send_back(wy).wait()
            tmp[32:64, :] = Q["bxr"][wy].astype(F32)
            for k in range(SHIFT):
                outf[k, 7 * wy + 3:7 * wy + 10, :] = tmp[32 + 7 * k:39 + 7 * k, :]
        bzcopy.wait()
        tmp[32:48, :] = Q["bzr"][...].astype(F32)
        for k in range(SHIFT):
            outf[k, 17:21, :] = tmp[32 + 4 * k:36 + 4 * k, :]
        out[...] = outf[:, 0:21, :].astype(BF)

        for c in fifth:
            c.wait()
        s16 = w2[0].astype(F32)
        for k in range(1, G2):
            s16 = s16 + w2[k].astype(F32)
        s16 = s16 * (1.0 / math.sqrt(tokens))
        right = jnp.concatenate([s16[48:64, 16 * g:16 * g + 16] for g in range(3)], axis=0)
        o_sum[:, 512:768] = jnp.concatenate([s16[0:48], right, jnp.zeros((C, 112), F32)], axis=1)

        for c in third:
            c.wait()
        for l in range(4):
            o_sum[:, 128 * l:128 * l + 128] = jnp.concatenate(
                [total[j // 2, 16 * (j % 2):16 * (j % 2) + 16, :] for j in range(3 * l, 3 * l + 3)], axis=0
            )

    return kernel


def deliver(back, sums, out, o_qkv, o_proj, o_up, o_down, o_head):
    out[...] = back[...]
    o_up[...] = sums[:, 0:192]
    o_down[...] = sums[:, 192:384]
    o_proj[...] = sums[:, 384:432]
    o_qkv[...] = sums[:, 512:656]
    col = sums[:, 384:512].T[48:49]
    o_head[...] = jnp.concatenate([-col, col], axis=0)


def body(features, labels, gain_one, gain_two, w_qkv, w_proj, w_up, w_down, w_head):
    nx, ny = lax.axis_size("gx"), lax.axis_size("gy")
    tokens = nx * ny * features.shape[0] * features.shape[1] * DEPTH
    vmem = pl.BlockSpec(memory_space=pltpu.VMEM)
    back, sums = pl.pallas_call(
        make_kernel(nx, ny, tokens),
        out_shape=[jax.ShapeDtypeStruct(features.shape, BF), jax.ShapeDtypeStruct((C, 768), F32)],
        in_specs=[vmem] * 9,
        out_specs=[vmem] * 2,
        scratch_shapes=list(scratch().values())
        + list(win_scratch().values()) * NP
        + list(tmp_scratch().values()) * NP
        + list(comm_scratch(nx, ny).values()),
        compiler_params=pltpu.CompilerParams(
            collective_id=0, has_side_effects=True, vmem_limit_bytes=60 * 2**20
        ),
    )(
        features, labels, w_qkv, w_proj, w_up, w_down.T, w_head.T,
        gain_one.reshape(1, C), gain_two.reshape(1, C),
    )
    out, d_qkv, d_proj, d_up, d_down, d_head = pl.pallas_call(
        deliver,
        out_shape=[jax.ShapeDtypeStruct(features.shape, BF)] + [
            jax.ShapeDtypeStruct(s, F32) for s in ((C, 144), (C, C), (C, FF), (C, FF), (2, C))
        ],
        in_specs=[vmem] * 2,
        out_specs=[vmem] * 6,
    )(back, sums)
    return out, d_qkv, d_proj, d_up, d_down.T, d_head.T


def solution(mesh):
    placed = (P("gx", "gy", None), P("gx", "gy", None), P(), P(), P(), P(), P(), P(), P())
    return jax.shard_map(
        body,
        mesh=mesh,
        in_specs=placed,
        out_specs=(P("gx", "gy", None), P(), P(), P(), P(), P()),
        check_vma=False,
    )
```

```python
import math

import jax
import jax.numpy as jnp
from jax import lax
from jax.experimental import pallas as pl
from jax.experimental.pallas import tpu as pltpu
from jax.sharding import PartitionSpec as P

BF = jnp.bfloat16
F32 = jnp.float32
C = 48
FF = 192
NH = 3
WIN = 7
SHIFT = 3
DEPTH = 42
WIDTH = DEPTH * C
LAB = 2048
LW = 2176
KP = 352
TL = 384
PT = 343
NZ = 6
NWY = 3
EPS = 1e-5
BIG = 2.0**100
LOG2E_4 = 0.25 * math.log2(math.e)
CH = [(0, 256), (256, 512), (512, 768), (768, 1024), (1024, 1152)]
GC1 = math.sqrt(2 / math.pi)
GC2 = 0.044715 * GC1
MESH = pl.DeviceIdType.MESH


def dot(a,b): return lax.dot_general(a,b,(((1,),(0,)),((),())),preferred_element_type=F32)
def dot_t(a,b): return lax.dot_general(a,b,(((1,),(1,)),((),())),preferred_element_type=F32)
def split3(v):
    a=v.astype(BF); r=v-a.astype(F32); b=r.astype(BF); r=r-b.astype(F32); return a,b,r.astype(BF)
def mean0(v): return jnp.sum(v,axis=0,keepdims=True)*(1.0/C)
def norm(v):
    s=v-mean0(v)
    r=lax.rsqrt(mean0(s*s)+EPS)
    return s*r, r
def norm_back(d,xh,r):
    return (d-mean0(d)-xh*mean0(d*xh))*r

def scratch():
    return dict(
      qkvT=pltpu.VMEM((144,C),BF), projT=pltpu.VMEM((C,C),BF), upT=pltpu.VMEM((FF,C),BF), downT=pltpu.VMEM((C,FF),BF), down=pltpu.VMEM((FF,C),BF),
      wx=pltpu.VMEM((128,512),BF), kmask=pltpu.VMEM((16,TL),BF), qmask=pltpu.VMEM((16,TL),F32),
      g1=pltpu.VMEM((C,1),F32), g2=pltpu.VMEM((C,1),F32), wd=pltpu.VMEM((C,1),F32),
      a_up=pltpu.VMEM((C,FF),F32), a_down=pltpu.VMEM((C,FF),F32), a_qkv=pltpu.VMEM((C,144),F32), a_proj=pltpu.VMEM((C,C),F32), a_head=pltpu.VMEM((C,128),F32),
    )
def win_scratch():
    return dict(oblk=pltpu.VMEM((256,2304),BF), P=pltpu.VMEM((KP,2304),BF),
       qt=pltpu.VMEM((2304,128),BF), ot=pltpu.VMEM((2304,128),BF), tokv=pltpu.VMEM((TL,256),BF), kT=pltpu.VMEM((96,TL),BF), n1=pltpu.VMEM((C,2*TL),BF))

def tmp_scratch():
    return dict(qblk=pltpu.VMEM((240,2304),BF), D=pltpu.VMEM((KP,2304),BF), dkv=pltpu.VMEM((TL,256),BF))

def init(S, Ws, Ts, wqkv, wproj, wup, wdownT, whT, g1, g2):
    S['qkvT'][...]=wqkv[...].T
    S['projT'][...]=wproj[...].T
    S['upT'][...]=wup[...].T
    S['downT'][...]=wdownT[...]
    S['down'][...]=wdownT[...].T
    wq=wqkv[...].astype(F32)
    wk=wq[:,48:96]; wv=wq[:,96:144]
    z=lambda n: jnp.zeros((C,n),F32)
    r=lax.broadcasted_iota(jnp.int32,(16,512),0); l=lax.broadcasted_iota(jnp.int32,(16,512),1)
    wqq=wq[:,0:48]
    rows_a=jnp.concatenate([wk,wk,z(160),wv,z(16),wqq,z(144)],axis=1)
    mask_a=((l==96+r)|((l>=304)&(l<307)&(r==7))).astype(F32)
    rows_b=jnp.concatenate([z(128),wk,wk,z(160),wqq,z(16),wv,z(16)],axis=1)
    mask_b=((l==224+r)|((l>=496)&(l<499)&(r==7))).astype(F32)
    S['wx'][...]=jnp.concatenate([rows_a,mask_a,rows_b,mask_b],axis=0).astype(BF)
    t=lax.broadcasted_iota(jnp.int32,(16,TL),1); r=lax.broadcasted_iota(jnp.int32,(16,TL),0)
    bz=(t>=4*49).astype(F32)
    u=t-49*sum((t>=49*k).astype(jnp.int32) for k in range(1,7))
    bx=(u>=28).astype(F32)
    v=u-7*sum((u>=7*k).astype(jnp.int32) for k in range(1,7))
    by=(v>=4).astype(F32)
    b=jnp.where(r<2,bx,jnp.where(r<4,by,bz))
    first=(r%2)==0
    S['kmask'][...]=jnp.where(r<6,jnp.where(first,1.0-b,b),jnp.where(r==6,(t>=343).astype(F32),(r==7).astype(F32))).astype(BF)
    S['qmask'][...]=jnp.where(r<6,jnp.where(first,b,1.0-b),(r==6).astype(F32))*(-BIG)
    wh=whT[...].astype(F32)
    cols=jnp.concatenate([g1[...],g2[...],wh[1:2]-wh[0:1],jnp.zeros((5,C),F32)],axis=0)
    cols=jnp.concatenate([cols,jnp.zeros((8,128-C),F32)],axis=1).T
    S['g1'][...]=cols[0:C,0:1]; S['g2'][...]=cols[0:C,1:2]; S['wd'][...]=cols[0:C,2:3]
    for k in ('a_up','a_down','a_qkv','a_proj','a_head'): S[k][...]=jnp.zeros(S[k].shape,F32)
    for w in Ws:
        w['oblk'][...]=jnp.zeros((256,2304),BF)
    for t in Ts:
        t['qblk'][...]=jnp.zeros((240,2304),BF)
        t['dkv'][...]=jnp.zeros((TL,256),BF)

def lane_mask(l0):
    lane=lax.broadcasted_iota(jnp.int32,(1,128),1)
    return jnp.where((lane>=l0)&(lane<l0+16),1.0,0.0).astype(BF)

def split2(v):
    a=v.astype(BF); return a,(v-a.astype(F32)).astype(BF)

def spread(parts):
    def block(j):
        c=j//2; k0=256*c//TL; k=j//3
        return parts[c][16*(k-k0):16*(k-k0)+16,128*(j%2):128*(j%2)+128]
    cols=[jnp.concatenate([block(3*k+i) for i in range(3)],axis=1) for k in range(6)]
    return jnp.concatenate([jnp.concatenate(cols[0:3],axis=0),jnp.concatenate(cols[3:6],axis=0)],axis=1)

def heads_of(c):
    return slice(16*(256*c//TL),16*((256*c+255)//TL)+16)

def window(out, x, sign, act, S, W, T, wproj, wup):
    x=x()
    g1=S['g1'][...]; g2=S['g2'][...]; wd=S['wd'][...]
    n1=(norm(x)[0]*g1).astype(BF)
    yield
    packT=dot(S['qkvT'][...],n1).astype(BF)
    yield
    km=S['kmask'][...]
    tok=dot(jnp.concatenate([n1[:,0:TL],km,n1[:,TL:],km],axis=0).T, S['wx'][...]).astype(BF)
    yield
    qs=split2(packT[0:48].astype(F32)*LOG2E_4)
    r=lax.broadcasted_iota(jnp.int32,(16,1),0)
    W['n1'][...]=n1
    W['tokv'][...]=tok[:,256:512]
    for w in range(2):
        W['kT'][48*w:48*w+48,:]=packT[48:96,TL*w:TL*w+TL]
    yield
    for w in range(2):
        sc=jnp.where(r<2,act[0],jnp.where(r<4,act[1],jnp.where(r<6,act[2+w],1.0)))
        qm=(S['qmask'][...]*sc).astype(BF)
        qtok=tok[:,256+128*w:384+128*w]
        for h in range(NH):
            k=3*w+h; ls=slice(k*TL,(k+1)*TL)
            for i in range(2):
                T['qblk'][128*w+48*i+16*h:128*w+48*i+16*h+16,ls]=qs[i][16*h:16*h+16,TL*w:TL*w+TL]
            T['qblk'][128*w+96:128*w+112,ls]=qm
            l0=64*(1-w)+16*h
            W['qt'][ls,:]=qtok*lane_mask(l0)
            yield
    tk=tok[:KP]
    vT=jnp.concatenate([packT[96:144,0:KP],packT[96:144,TL:TL+KP]],axis=0)
    def fwd_dot(c):
        rs=slice(0,112) if c<4 else (slice(0,240) if c==4 else slice(128,240))
        return jnp.exp2(dot(tk[:,rs],T['qblk'][rs,256*c:256*c+256]))
    mixp=[]
    p=fwd_dot(0)
    for c in range(9):
        yield
        nxt=fwd_dot(c+1) if c<8 else None
        P=(p*(1.0/jnp.sum(p,axis=0,keepdims=True))).astype(BF)
        W['P'][:,256*c:256*c+256]=P
        yield
        mixp.append(dot(vT[heads_of(c)],P))
        p=nxt
    mixf=spread(mixp)
    mixed=mixf.astype(BF)
    ao=dot(S['projT'][...],mixed).astype(BF).astype(F32)
    yield
    state=(x+ao).astype(BF).astype(F32)
    xh2,r2=norm(state)
    n2=(xh2*g2).astype(BF)
    yield
    hh=dot(S['upT'][...],n2)
    yield
    h2=hh*hh
    t=jnp.tanh(hh*(GC1+GC2*h2))
    s=0.5+0.5*t
    inf=hh*s
    inner=inf.astype(BF)
    dg=s+inf*(1.0-s)*(2*GC1+6*GC2*h2)
    yield
    res=(state+dot(S['downT'][...],inner)).astype(BF).astype(F32)
    yield
    z=jnp.sum(res*wd,axis=0,keepdims=True)
    g=sign*(1.0/(1.0+jnp.exp(-z*sign)))
    rg=res*g
    S['a_head'][...]+=sum(rg[:,128*i:128*i+128] for i in range(1,6))+rg[:,0:128]
    dres=(wd*g).astype(BF)
    yield
    dinner=dot(S['down'][...],dres).astype(BF).astype(F32)
    yield
    S['a_down'][...]+=dot_t(dres,inner)
    yield
    dh=(dinner*dg).astype(BF)
    yield
    S['a_up'][...]+=dot_t(n2,dh)
    yield
    dn2=dot(wup[...],dh).astype(BF).astype(F32)
    yield
    dst=(dres.astype(F32)+norm_back(dn2*g2,xh2,r2)).astype(BF)
    yield
    S['a_proj'][...]+=dot_t(mixed,dst)
    yield
    dO=dot(wproj[...],dst).astype(BF)
    yield
    zr=jnp.zeros((16,TL),BF)
    dOtok=jnp.concatenate([dO[:,TL:],zr,dO[:,0:TL],zr],axis=0).T
    yield
    pr=mixf*dO.astype(F32)
    r16=lax.broadcasted_iota(jnp.int32,(16,TL),0)
    for w in range(2):
        for h in range(NH):
            k=3*w+h; ls=slice(k*TL,(k+1)*TL); ws=slice(TL*w,TL*w+TL); o=192*w
            d0,d1,d2=split3(-jnp.sum(pr[16*h:16*h+16,ws],axis=0,keepdims=True))
            W['oblk'][o+16*h:o+16*h+16,ls]=dO[16*h:16*h+16,ws]
            W['oblk'][o+48:o+64,ls]=jnp.where(r16==0,d0.astype(F32),jnp.where(r16==1,d1.astype(F32),jnp.where(r16==2,d2.astype(F32),0.0))).astype(BF)
            l0=64*(1-w)+16*h
            W['ot'][ls,:]=dOtok*lane_mask(l0)
            yield
    out(dst)

def backward(out, S, W, T):
    def bwd_dot(c):
        rs=slice(0,64) if c<4 else (slice(0,256) if c==4 else slice(128,256))
        return dot(W['tokv'][0:KP,rs],W['oblk'][rs,256*c:256*c+256]).astype(BF)
    dqp=[]
    dp=bwd_dot(0)
    for c in range(9):
        yield
        nxt=bwd_dot(c+1) if c<8 else None
        cs=slice(256*c,256*c+256)
        ds=W['P'][:,cs]*dp
        T['D'][:,cs]=ds
        yield
        dqp.append(dot(W['kT'][heads_of(c),0:KP],ds))
        dp=nxt
    dq=(0.25*spread(dqp)).astype(BF)
    yield
    def over_queries(a,b):
        t=None
        for i in range(3):
            ks=slice(768*i,768*i+768)
            d=dot(a[:,ks],b[ks,:])
            t=d if t is None else t+d
            yield t
    for t in over_queries(W['P'],W['ot']):
        yield
    T['dkv'][0:KP,128:256]=t.astype(BF)
    for t in over_queries(T['D'],W['qt']):
        yield
    T['dkv'][0:KP,0:128]=(0.25*t).astype(BF)
    yield
    dk=T['dkv'][:,0:128].T; dv=T['dkv'][:,128:256].T
    dpack=jnp.concatenate([dq,jnp.concatenate([dk[64:112],dk[0:48]],axis=1),jnp.concatenate([dv[64:112],dv[0:48]],axis=1)],axis=0)
    yield
    S['a_qkv'][...]+=dot_t(W['n1'][...],dpack)
    out(dpack)

def finish(x, dpack, dst, S, wqkv):
    g1=S['g1'][...]
    xh1,r1=norm(x)
    dn1=dot(wqkv[...],dpack).astype(BF).astype(F32)
    return (dst.astype(F32)+norm_back(dn1*g1,xh1,r1)).astype(BF)


def drive(timed):
    t=0
    live=list(timed)
    while live:
        left=[]
        for start,g in live:
            if t>=start:
                try:
                    next(g)
                except StopIteration:
                    continue
            left.append((start,g))
        live=left
        t+=1


G1 = 8
G2 = 16
ROWS = 32
TWO = sorted(
    ((a, b) for a in range(4) for b in range(4) if a or b), key=lambda s: -sum(min(v, 4 - v) for v in s)
)
NP = 3
IN_KEYS = ("i_feat", "i_lab", "i_qkv", "i_proj", "i_up", "i_down", "i_head", "i_g1", "i_g2")
S_KEYS = tuple(scratch())
W_KEYS = tuple(win_scratch())
T_KEYS = tuple(tmp_scratch())


def comm_scratch(nx, ny):
    return dict(
        i_feat=pltpu.VMEM((WIN, 21, WIDTH), BF),
        i_lab=pltpu.VMEM((WIN, 21, DEPTH), jnp.int32),
        i_qkv=pltpu.VMEM((C, 144), BF),
        i_proj=pltpu.VMEM((C, C), BF),
        i_up=pltpu.VMEM((C, FF), BF),
        i_down=pltpu.VMEM((C, FF), BF),
        i_head=pltpu.VMEM((2, C), BF),
        i_g1=pltpu.VMEM((1, C), F32),
        i_g2=pltpu.VMEM((1, C), F32),
        ins=pltpu.SemaphoreType.DMA((10,)),
        grid=pltpu.VMEM((WIN, 24, LW), F32),
        rows=pltpu.VMEM((NWY, 64, LW), F32),
        xs=pltpu.VMEM((NWY, 32, LW), BF),
        xr=pltpu.VMEM((NWY, 32, LW), BF),
        ys=pltpu.VMEM((16, LW), BF),
        yr=pltpu.VMEM((16, LW), BF),
        ds=pltpu.VMEM((16, LW), BF),
        dr=pltpu.VMEM((16, LW), BF),
        xwin=pltpu.VMEM((NWY * NP, C, 2 * TL), BF),
        dpk=pltpu.VMEM((NWY * NP, 3 * C, 2 * TL), BF),
        dst=pltpu.VMEM((NWY * NP, C, 2 * TL), BF),
        sg=pltpu.VMEM((8, 2 * TL), F32),
        zt=pltpu.VMEM((LAB, 128), BF),
        back=pltpu.VMEM((NWY, 64, WIDTH), F32),
        bxs=pltpu.VMEM((NWY, 32, WIDTH), BF),
        bxr=pltpu.VMEM((NWY, 32, WIDTH), BF),
        bzs=pltpu.VMEM((16, WIDTH), BF),
        bzr=pltpu.VMEM((16, WIDTH), BF),
        bys=pltpu.VMEM((16, WIDTH), BF),
        byr=pltpu.VMEM((16, WIDTH), BF),
        bds=pltpu.VMEM((16, WIDTH), BF),
        bdr=pltpu.VMEM((16, WIDTH), BF),
        tmp=pltpu.VMEM((64, WIDTH), F32),
        outf=pltpu.VMEM((WIN, 24, WIDTH), F32),
        part=pltpu.VMEM((G1, ROWS, 128), F32),
        r1=pltpu.VMEM((G1 - 1, ROWS, 128), F32),
        r2=pltpu.VMEM((G2, ROWS, 128), BF),
        total=pltpu.VMEM((G1, ROWS, 128), F32),
        w1=pltpu.VMEM((G1, 64, 128), BF),
        w2=pltpu.VMEM((G2, 64, 128), BF),
        hs=pltpu.SemaphoreType.DMA((NWY + 2,)),
        hr=pltpu.SemaphoreType.DMA((NWY + 2,)),
        bs=pltpu.SemaphoreType.DMA((NWY + 2,)),
        br=pltpu.SemaphoreType.DMA((NWY + 2,)),
        s1=pltpu.SemaphoreType.DMA((G1 - 1,)),
        q1=pltpu.SemaphoreType.DMA((G1 - 1,)),
        s2=pltpu.SemaphoreType.DMA((G2 - 1,)),
        q2=pltpu.SemaphoreType.DMA((G2 - 1,)),
        s3=pltpu.SemaphoreType.DMA((G1 - 1,)),
        q3=pltpu.SemaphoreType.DMA((G1 - 1,)),
        u1=pltpu.SemaphoreType.DMA((G1 - 1,)),
        v1=pltpu.SemaphoreType.DMA((G1 - 1,)),
        u2=pltpu.SemaphoreType.DMA((G2 - 1,)),
        v2=pltpu.SemaphoreType.DMA((G2 - 1,)),
    )


def remote(src, dst, ssem, rsem, to):
    return pltpu.make_async_remote_copy(
        src_ref=src, dst_ref=dst, send_sem=ssem, recv_sem=rsem, device_id=to, device_id_type=MESH
    )


def make_kernel(nx, ny, tokens):
    c_keys = tuple(comm_scratch(nx, ny))

    def kernel(*refs):
        hbm = refs[:9]
        refs = refs[9:]
        out, o_sum = refs[:2]
        refs = refs[2:]
        S = dict(zip(S_KEYS, refs))
        refs = refs[len(S_KEYS):]
        Ws = [dict(zip(W_KEYS, refs[i * len(W_KEYS):])) for i in range(NP)]
        refs = refs[NP * len(W_KEYS):]
        Ts = [dict(zip(T_KEYS, refs[i * len(T_KEYS):])) for i in range(NP)]
        Q = dict(zip(c_keys, refs[NP * len(T_KEYS):]))
        held = [Q[k] for k in IN_KEYS]
        feat, lab, wqkv, wproj, wup, wdown, whead, g1, g2 = held
        mx = lax.axis_index("gx")
        my = lax.axis_index("gy")

        def at(dx, dy):
            return (lax.rem(mx + dx + nx, nx), lax.rem(my + dy + ny, ny))

        half = lax.rem(lax.div(mx, 2), 2)
        core = lax.rem(mx, 2)
        px = lax.div(mx, 4)
        m1 = px * 2 + core
        m2 = half * ny + my

        def in_one(k):
            x2 = lax.rem(px + k // 2, 4)
            c2 = lax.rem(core + k % 2, 2)
            return x2 * 2 + c2, ((x2 * 2 + half) * 2 + c2, my)

        z = half * 2 + lax.div(my, 4)
        y = lax.rem(my, 4)

        def in_two(k):
            dz, dy = TWO[k - 1]
            z2, y2 = lax.rem(z + dz, 4), lax.rem(y + dy, 4)
            return ((px * 2 + lax.div(z2, 2)) * 2 + core, lax.rem(z2, 2) * 4 + y2)

        barrier = pltpu.get_barrier_semaphore()
        peers = [at(1, 0), at(-1, 0), at(1, 1), at(-1, -1)]
        peers += [in_one(k)[1] for k in range(1, G1)] + [in_two(k) for k in range(1, G2)]
        for p in peers:
            pl.semaphore_signal(barrier, inc=1, device_id=p, device_id_type=MESH)

        ins = Q["ins"]
        early = [
            pltpu.make_async_copy(hbm[0].at[0:SHIFT], feat.at[0:SHIFT], ins.at[0]),
            pltpu.make_async_copy(hbm[1], lab, ins.at[1]),
        ]
        late = [pltpu.make_async_copy(hbm[0].at[SHIFT:WIN], feat.at[SHIFT:WIN], ins.at[2])]
        late += [pltpu.make_async_copy(hbm[i], held[i], ins.at[i + 1]) for i in range(2, 9)]
        for c in early + late:
            c.start()

        grid = Q["grid"]
        tmp = Q["rows"]

        def widen(x0, x1):
            n = x1 - x0
            grid[x0:x1, 0:21, 0:WIDTH] = feat[x0:x1].astype(F32)
            grid[x0:x1, 0:21, WIDTH:LAB] = jnp.zeros((n, 21, LAB - WIDTH), F32)
            grid[x0:x1, 0:21, LAB:LW] = jnp.zeros((n, 21, LW - LAB), F32)
            grid[x0:x1, 0:21, LAB:LAB + DEPTH] = lab[x0:x1].astype(F32)

        def pack(wy):
            n = WIN if wy < 2 else 4
            for k in range(SHIFT):
                tmp[wy, 7 * k:7 * k + n, :] = grid[k, 7 * wy + 3:7 * wy + 3 + n, :]
            Q["xs"][wy] = tmp[wy, 0:32, :].astype(BF)

        hs, hr = Q["hs"], Q["hr"]
        xcopy = [remote(Q["xs"].at[w], Q["xr"].at[w], hs.at[w], hr.at[w], at(-1, 0)) for w in range(NWY)]
        ycopy = remote(Q["ys"], Q["yr"], hs.at[3], hr.at[3], at(0, -1))
        dcopy = remote(Q["ds"], Q["dr"], hs.at[4], hr.at[4], at(-1, -1))
        for c in early:
            c.wait()
        widen(0, SHIFT)
        pack(0)
        pl.semaphore_wait(barrier, len(peers))
        xcopy[0].start()
        for c in late:
            c.wait()
        widen(SHIFT, WIN)
        pack(1)
        pack(2)
        for k in range(4):
            tmp[0, 3 * k:3 * k + 3, :] = grid[3 + k, 0:3, :]
        Q["ys"][...] = tmp[0, 0:16, :].astype(BF)
        for k in range(SHIFT):
            tmp[1, 3 * k:3 * k + 3, :] = grid[k, 0:3, :]
        Q["ds"][...] = tmp[1, 0:16, :].astype(BF)

        init(S, Ws, Ts, wqkv, wproj, wup, wdown, whead, g1, g2)
        rows = Q["rows"]
        for wy in range(NWY):
            n = WIN if wy < 2 else 4
            for k in range(4):
                rows[wy, 7 * k:7 * k + n, :] = grid[3 + k, 7 * wy + 3:7 * wy + 3 + n, :]
            rows[wy, 48:64, :] = jnp.zeros((16, LW), F32)
        Q["zt"][...] = jnp.zeros((LAB, 128), BF)

        act_x = (mx == nx - 1).astype(F32)
        last_y = my == ny - 1
        lanes = lax.broadcasted_iota(jnp.int32, (1, TL), 1)

        xcopy[0].wait()
        xcopy[1].start()
        xcopy[2].start()
        ycopy.start()
        dcopy.start()

        def send_back(w):
            return remote(Q["bxs"].at[w], Q["bxr"].at[w], Q["bs"].at[w], Q["br"].at[w], at(1, 0))

        def tail(w):
            for p in range(NP):
                v = finish(Q["xwin"][NP * w + p].astype(F32), Q["dpk"][NP * w + p], Q["dst"][NP * w + p], S, wqkv)
                for i in range(2):
                    for j in range(WIN):
                        z = (7 * (2 * p + i) + j + SHIFT) % DEPTH
                        Q["zt"][C * z:C * z + C, 0:49] = v[:, TL * i + 49 * j:TL * i + 49 * j + 49]
                    yield
            flat = Q["zt"][...].T.astype(F32)[0:64, 0:WIDTH]
            Q["back"][w] = flat
            yield
            Q["bxs"][w] = jnp.concatenate([flat[28:49], jnp.zeros((11, WIDTH), F32)], axis=0).astype(BF)

        def windows_of(w):
            cols = rows[w].astype(BF).T
            zero = jnp.zeros((C, TL - PT), BF)
            zrow = jnp.zeros((1, TL - PT), F32)
            for p in range(NP):
                zs = [[(7 * wz + j + SHIFT) % DEPTH for j in range(WIN)] for wz in (2 * p, 2 * p + 1)]
                halves = [jnp.concatenate([cols[C * z:C * z + C, 0:49] for z in u] + [zero], axis=1) for u in zs]
                Q["xwin"][NP * w + p] = jnp.concatenate(halves, axis=1)
                marks = [
                    jnp.concatenate([cols[LAB + z:LAB + z + 1, 0:49].astype(F32) for z in u] + [zrow], axis=1)
                    for u in zs
                ]
                Q["sg"][p:p + 1, :] = jnp.concatenate(
                    [jnp.where(lanes < PT, 1.0 - 2.0 * m, 0.0) for m in marks], axis=1
                )
                yield

        rows[0, 28:49, :] = Q["xr"][0].astype(F32)[0:21]
        drive([(0, windows_of(0))])

        part = Q["part"]

        def scatter():
            copies = []
            for k in range(1, G1):
                slot, to = in_one(k)
                copies.append(remote(part.at[slot], Q["r1"].at[k - 1], Q["s1"].at[k - 1], Q["q1"].at[k - 1], to))
            return copies

        def first_sums():
            a_head = jnp.sum(S["a_head"][...], axis=1, keepdims=True)
            acc = jnp.concatenate(
                [S["a_up"][...], S["a_down"][...], S["a_proj"][...], a_head, jnp.zeros((C, 79), F32)], axis=1
            )
            for j in range(16):
                if j < 12:
                    v = acc[16 * (j % 3):16 * (j % 3) + 16, 128 * (j // 3):128 * (j // 3) + 128]
                else:
                    v = jnp.zeros((16, 128), F32)
                part[j // 2, 16 * (j % 2):16 * (j % 2) + 16, :] = v

        def step(wy, _):
            gens, later = [], []
            act_y = jnp.logical_and(last_y, wy == 2).astype(F32)
            for p in range(NP):
                def put_dst(dst, p=p):
                    Q["dst"][NP * wy + p] = dst

                def put_dpk(dpack, p=p):
                    Q["dpk"][NP * wy + p] = dpack

                def get(p=p):
                    return Q["xwin"][NP * wy + p].astype(F32)

                act = (act_x, act_y, F32(0.0), F32(1.0 if p == NP - 1 else 0.0))
                gens.append((p, window(put_dst, get, Q["sg"][p:p + 1, :], act, S, Ws[p], Ts[p], wproj, wup)))
                later.append((p, backward(put_dpk, S, Ws[p], Ts[p])))
            before = lax.rem(wy + 2, 3)
            drive(gens + [(6, tail(before))])

            @pl.when(wy > 0)
            def _():
                send_back(before).start()

            @pl.when(wy == 2)
            def _():
                first_sums()
                for c in scatter():
                    c.start()

            following = lax.rem(wy + 1, 3)

            @pl.when(wy < 2)
            def _():
                remote(
                    Q["xs"].at[following], Q["xr"].at[following], hs.at[following], hr.at[following], at(-1, 0)
                ).wait()
                rows[following, 28:49, :] = Q["xr"][following].astype(F32)[0:21]

            @pl.when(wy == 1)
            def _():
                ycopy.wait()
                dcopy.wait()
                Q["tmp"][0:16, :] = Q["yr"][:, 0:WIDTH].astype(F32)
                Q["tmp"][16:32, :] = Q["dr"][:, 0:WIDTH].astype(F32)
                yl = Q["yr"][:, LAB:LW].astype(F32)
                dl = Q["dr"][:, LAB:LW].astype(F32)
                for k in range(4):
                    rows[2, 7 * k + 4:7 * k + 7, 0:WIDTH] = Q["tmp"][3 * k:3 * k + 3, :]
                    rows[2, 7 * k + 4:7 * k + 7, LAB:LW] = yl[3 * k:3 * k + 3]
                for k in range(SHIFT):
                    rows[2, 28 + 7 * k + 4:28 + 7 * k + 7, 0:WIDTH] = Q["tmp"][16 + 3 * k:16 + 3 * k + 3, :]
                    rows[2, 28 + 7 * k + 4:28 + 7 * k + 7, LAB:LW] = dl[3 * k:3 * k + 3]

            drive(later + [(4, windows_of(following))])
            return 0

        lax.fori_loop(0, NWY, step, 0)

        w1, w2 = Q["w1"], Q["w2"]
        mine = S["a_qkv"][...].astype(BF)
        edge = jnp.concatenate(
            [mine[16 * g:16 * g + 16, 128:144] for g in range(3)] + [jnp.zeros((16, 80), BF)], axis=1
        )
        w1[m1] = jnp.concatenate([mine[:, 0:128], edge], axis=0)
        fourth = [
            remote(w1.at[m1], w1.at[m1], Q["u1"].at[k - 1], Q["v1"].at[k - 1], in_one(k)[1]) for k in range(1, G1)
        ]
        for c in fourth:
            c.start()

        for c in scatter():
            c.wait()
        csum = part[m1]
        for k in range(G1 - 1):
            csum = csum + Q["r1"][k]
        r2 = Q["r2"]
        r2[m2] = csum.astype(BF)
        second = [
            remote(r2.at[m2], r2.at[m2], Q["s2"].at[k - 1], Q["q2"].at[k - 1], in_two(k)) for k in range(1, G2)
        ]
        for c in second:
            c.start()

        drive([(0, tail(2))])
        back, tmp = Q["back"], Q["tmp"]
        for k in range(4):
            tmp[3 * k:3 * k + 3, :] = back[2, 7 * k + 4:7 * k + 7, :]
        for k in range(SHIFT):
            tmp[16 + 3 * k:16 + 3 * k + 3, :] = back[2, 28 + 7 * k + 4:28 + 7 * k + 7, :]
        for k in range(SHIFT):
            tmp[32 + 4 * k:36 + 4 * k, :] = back[2, 28 + 7 * k:28 + 7 * k + 4, :]
        Q["bzs"][...] = tmp[32:48, :].astype(BF)
        bzcopy = remote(Q["bzs"], Q["bzr"], Q["bs"].at[2], Q["br"].at[2], at(1, 0))
        Q["bys"][...] = tmp[0:16, :].astype(BF)
        Q["bds"][...] = tmp[16:32, :].astype(BF)
        bycopy = remote(Q["bys"], Q["byr"], Q["bs"].at[3], Q["br"].at[3], at(0, 1))
        bdcopy = remote(Q["bds"], Q["bdr"], Q["bs"].at[4], Q["br"].at[4], at(1, 1))
        bzcopy.start()
        bycopy.start()
        bdcopy.start()

        for c in fourth:
            c.wait()
        s8 = w1[0].astype(F32)
        for k in range(1, G1):
            s8 = s8 + w1[k].astype(F32)
        w2[m2] = s8.astype(BF)
        fifth = [
            remote(w2.at[m2], w2.at[m2], Q["u2"].at[k - 1], Q["v2"].at[k - 1], in_two(k)) for k in range(1, G2)
        ]
        for c in fifth:
            c.start()

        outf = Q["outf"]
        for x in range(SHIFT, WIN):
            k = x - SHIFT
            for wy in range(NWY):
                n = WIN if wy < 2 else 4
                outf[x, 7 * wy + 3:7 * wy + 3 + n, :] = back[wy, 7 * k:7 * k + n, :]

        for c in second:
            c.wait()
        ctot = r2[0].astype(F32)
        for k in range(1, G2):
            ctot = ctot + r2[k].astype(F32)
        total = Q["total"]
        total[m1] = ctot * (1.0 / math.sqrt(tokens))
        third = [
            remote(total.at[m1], total.at[m1], Q["s3"].at[k - 1], Q["q3"].at[k - 1], in_one(k)[1])
            for k in range(1, G1)
        ]
        for c in third:
            c.start()

        bycopy.wait()
        bdcopy.wait()
        tmp[0:16, :] = Q["byr"][...].astype(F32)
        tmp[16:32, :] = Q["bdr"][...].astype(F32)
        for k in range(4):
            outf[SHIFT + k, 0:3, :] = tmp[3 * k:3 * k + 3, :]
        for k in range(SHIFT):
            outf[k, 0:3, :] = tmp[16 + 3 * k:16 + 3 * k + 3, :]
        for wy in range(2):
            send_back(wy).wait()
            tmp[32:64, :] = Q["bxr"][wy].astype(F32)
            for k in range(SHIFT):
                outf[k, 7 * wy + 3:7 * wy + 10, :] = tmp[32 + 7 * k:39 + 7 * k, :]
        bzcopy.wait()
        tmp[32:48, :] = Q["bzr"][...].astype(F32)
        for k in range(SHIFT):
            outf[k, 17:21, :] = tmp[32 + 4 * k:36 + 4 * k, :]
        out[...] = outf[:, 0:21, :].astype(BF)

        for c in fifth:
            c.wait()
        s16 = w2[0].astype(F32)
        for k in range(1, G2):
            s16 = s16 + w2[k].astype(F32)
        s16 = s16 * (1.0 / math.sqrt(tokens))
        right = jnp.concatenate([s16[48:64, 16 * g:16 * g + 16] for g in range(3)], axis=0)
        o_sum[:, 512:768] = jnp.concatenate([s16[0:48], right, jnp.zeros((C, 112), F32)], axis=1)

        for c in third:
            c.wait()
        for l in range(4):
            o_sum[:, 128 * l:128 * l + 128] = jnp.concatenate(
                [total[j // 2, 16 * (j % 2):16 * (j % 2) + 16, :] for j in range(3 * l, 3 * l + 3)], axis=0
            )

    return kernel


def deliver(back, sums, out, o_qkv, o_proj, o_up, o_down, o_head):
    out[...] = back[...]
    o_up[...] = sums[:, 0:192]
    o_down[...] = sums[:, 192:384]
    o_proj[...] = sums[:, 384:432]
    o_qkv[...] = sums[:, 512:656]
    col = sums[:, 384:512].T[48:49]
    o_head[...] = jnp.concatenate([-col, col], axis=0)


def body(features, labels, gain_one, gain_two, w_qkv, w_proj, w_up, w_down, w_head):
    nx, ny = lax.axis_size("gx"), lax.axis_size("gy")
    tokens = nx * ny * features.shape[0] * features.shape[1] * DEPTH
    vmem = pl.BlockSpec(memory_space=pltpu.VMEM)
    back, sums = pl.pallas_call(
        make_kernel(nx, ny, tokens),
        out_shape=[jax.ShapeDtypeStruct(features.shape, BF), jax.ShapeDtypeStruct((C, 768), F32)],
        in_specs=[pl.BlockSpec(memory_space=pl.ANY)] * 9,
        out_specs=[vmem] * 2,
        scratch_shapes=list(scratch().values())
        + list(win_scratch().values()) * NP
        + list(tmp_scratch().values()) * NP
        + list(comm_scratch(nx, ny).values()),
        compiler_params=pltpu.CompilerParams(
            collective_id=0, has_side_effects=True, vmem_limit_bytes=60 * 2**20
        ),
    )(
        features, labels, w_qkv, w_proj, w_up, w_down.T, w_head.T,
        gain_one.reshape(1, C), gain_two.reshape(1, C),
    )
    out, d_qkv, d_proj, d_up, d_down, d_head = pl.pallas_call(
        deliver,
        out_shape=[jax.ShapeDtypeStruct(features.shape, BF)] + [
            jax.ShapeDtypeStruct(s, F32) for s in ((C, 144), (C, C), (C, FF), (C, FF), (2, C))
        ],
        in_specs=[vmem] * 2,
        out_specs=[vmem] * 6,
    )(back, sums)
    return out, d_qkv, d_proj, d_up, d_down.T, d_head.T


def solution(mesh):
    placed = (P("gx", "gy", None), P("gx", "gy", None), P(), P(), P(), P(), P(), P(), P())
    return jax.shard_map(
        body,
        mesh=mesh,
        in_specs=placed,
        out_specs=(P("gx", "gy", None), P(), P(), P(), P(), P()),
        check_vma=False,
    )
```
